128 devices in a mesh: tm: 8 (over y, core), band: 16 (over x, z).
Axes of the slice: x: 4, y: 4, z: 4, core: 2. Of those that a mesh axis runs over, the one named last changes fastest.
Arguments:
- strain_rate: bfloat16 [32, 4096, 256], P('tm', 'band'), may hold values from -6 to 6
- pair_table: int32 [16, 8, 4], replicated, may hold values from 0 to 128, as said below
- pair_count: int32 [16], replicated, may hold values from 1 to 8, 64 in all
Outputs:
- xcorr: bfloat16 [16, 8, 256, 128, 128], P('band', 'tm')
The draws below stay inside these ranges and needn't reach their ends.
Inputs may be any that keep to these rules, and one draw needn't show every extreme that they name: `pair_table`: columns 0 and 1 are blocks i and j with |i - j| <= 4; columns 2 and 3 are lo and hi with 1 <= lo < 16 and 96 <= hi <= 128; each owner's first slot has hi = 128. Slots at or past an owner's count hold valid entries too. Owner b's live slots are its first pair_count[b] slots; the counts sum to 64 and the largest equals 8.
All inputs are finite; a program needn't handle non-finite values.
Results may differ from the reference program's by a relative error of at most 0.0077.
Values may be sent and summed in bfloat16 or wider, within the bound.
A program may use at most 128 MiB of HBM per device.

```python
import math
import jax
import jax.numpy as jnp
import numpy as np
from jax import lax

L = 256
F = 128
BLK = 128
NBLK = 32
CH = 4096
SUB = 64
REACH = 4
SEG = 32
PCAP = 8
LIVE = 64
N_BAND = 16


def draw_pair_table(key, part):
    key = jax.random.fold_in(key, 11)
    home_key, step_key, low_key, high_key = jax.random.split(key, 4)
    grid_shape = (N_BAND, PCAP)
    home_block = jax.random.randint(home_key, grid_shape, 0, NBLK)
    home_block = home_block.at[0, 0].set(0)
    offsets = jax.random.randint(step_key, grid_shape, -REACH, REACH + 1)
    near_block = jnp.clip(home_block + offsets, 0, NBLK - 1)
    low_bin = jax.random.randint(low_key, grid_shape, 1, F // 8)
    high_bin = jax.random.randint(high_key, grid_shape, F - F // 4, F + 1)
    high_bin = high_bin.at[:, 0].set(F)
    return jnp.stack([home_block, near_block, low_bin, high_bin], axis=-1).astype(jnp.int32)


def levels(key, extent, shards, least, high):
    factor_of = 1.0
    for axis_at, blocks in shards:
        heights = jax.random.uniform(jax.random.fold_in(jax.random.fold_in(key, 6), axis_at), (blocks,), jnp.float32, least / len(shards), high / len(shards))
        factor_of = factor_of * jnp.repeat(jnp.exp(heights), extent[axis_at] // blocks).reshape((-1,) + (1,) * (len(extent) - 1 - axis_at))
    return factor_of


def profile(amount, total, most, slope):
    weights = [(1 << 20) // math.isqrt(grade ** slope) + 1 for grade in range(2, amount + 1)]
    rest, holding = total - most - (amount - 1), [1] * (amount - 1)
    while rest > 0:
        free = [i for i in range(amount - 1) if holding[i] < most]
        mass, remaining = sum([weights[i] for i in free]), rest
        for i in free:
            extra = min(most - holding[i], max(1, remaining * weights[i] // mass), rest)
            holding[i] = holding[i] + extra
            rest = rest - extra
    return np.array([most] + holding)


def ragged(stream_key, amount, total, bound, lean):
    if amount == 2:
        one = jax.random.randint(stream_key, (), max(1, total - bound), min(bound, total - 1) + 1)
        return jnp.stack([one, total - one])
    lengths = jnp.asarray(profile(amount, total, bound, lean), jnp.int32)
    couples = (amount - 1) // 2
    giver, taker = lengths[1:1 + 2 * couples:2], lengths[2:2 + 2 * couples:2]
    room = jnp.minimum(giver - 1, bound - taker)
    shifted = jax.random.randint(jax.random.fold_in(stream_key, 1), (couples,), 0, 1 << 20) % (room + 1)
    lengths = lengths.at[1:1 + 2 * couples:2].set(giver - shifted).at[2:2 + 2 * couples:2].set(taker + shifted)
    return lengths[jax.random.permutation(jax.random.fold_in(stream_key, 2), amount)]


def normal_values(own_key, shape, spread, most, cuts=(), kind=jnp.bfloat16):
    loudness = levels(own_key, shape, cuts, -0.22, 0.18) if cuts else 1.0
    drawn = jax.random.normal(own_key, shape, jnp.float32) * spread * loudness
    return jnp.minimum(jnp.maximum(drawn, -most), most).astype(kind)


def setup_inputs(seed: int = 0) -> dict:
    seeds = jax.random.split(jax.random.key(seed), 4)
    strain_rate = normal_values(seeds[0], (SEG, CH, L), 1.0, 6.0, ((0, 8), (1, 16)))
    pair_table = draw_pair_table(jax.random.fold_in(seeds[3], 71), 0)
    pair_count = ragged(seeds[2], N_BAND, LIVE, PCAP, 2).astype(jnp.int32)
    return dict(strain_rate=strain_rate, pair_table=pair_table, pair_count=pair_count)


EPSILON = 1e-06

def forward_table(samples):
    position = jnp.arange(samples, dtype=jnp.int32)[:, None]
    harmonic = jnp.arange(samples // 2, dtype=jnp.int32)[None, :]
    angles = (position * harmonic % samples).astype(jnp.float32) * (2.0 * math.pi / samples)
    factor = 1.0 / math.sqrt(samples)
    return jnp.stack([jnp.cos(angles) * factor, -jnp.sin(angles) * factor], axis=1).astype(jnp.bfloat16)

def inverse_table(frequency, samples):
    delays = jnp.arange(samples, dtype=jnp.int32)[None, :]
    angles = (frequency[:, None] * delays % samples).astype(jnp.float32) * (2.0 * math.pi / samples)
    factor = 2.0 / math.sqrt(samples // 2)
    return jnp.stack([jnp.cos(angles) * factor, -jnp.sin(angles) * factor], axis=1).astype(jnp.bfloat16)

def reference(strain_rate, pair_table, pair_count):
    spectrum = jnp.einsum('scl,lrk->scrk', strain_rate.astype(jnp.float32), forward_table(L).astype(jnp.float32))
    spectral_power = lax.optimization_barrier(jnp.sum(spectrum * spectrum, axis=2))
    band_level = lax.optimization_barrier(jnp.mean(spectral_power.reshape(SEG, CH, F // SUB, SUB), axis=-1))
    whitened = spectrum.reshape(SEG, CH, 2, F // SUB, SUB) / jnp.sqrt(band_level + EPSILON)[:, :, None, :, None]
    whitened = whitened.reshape(SEG, CH, 2, F).astype(jnp.bfloat16)
    blocks = whitened.reshape(SEG, NBLK, BLK, 2, F)
    live_slots = (jnp.arange(PCAP, dtype=jnp.int32)[None, :] < pair_count[:, None]).astype(jnp.float32)
    inverse = inverse_table(jnp.arange(F, dtype=jnp.int32), L).astype(jnp.float32)
    bin_index = jnp.arange(F, dtype=jnp.int32)

    def one_slot(slot_args):
        slot_pair, live_flag = slot_args
        left_block = lax.dynamic_index_in_dim(blocks, slot_pair[0], 1, keepdims=False).astype(jnp.float32)
        right_block = lax.dynamic_index_in_dim(blocks, slot_pair[1], 1, keepdims=False).astype(jnp.float32)
        real_part = jnp.einsum('sak,sbk->kab', left_block[:, :, 0], right_block[:, :, 0]) + jnp.einsum('sak,sbk->kab', left_block[:, :, 1], right_block[:, :, 1])
        imag_part = jnp.einsum('sak,sbk->kab', left_block[:, :, 1], right_block[:, :, 0]) - jnp.einsum('sak,sbk->kab', left_block[:, :, 0], right_block[:, :, 1])
        inside = ((slot_pair[2] <= bin_index) & (bin_index < slot_pair[3])).astype(jnp.float32) * (live_flag / SEG)
        cross_spec = (jnp.stack([real_part, imag_part], 1) * inside[:, None, None, None]).astype(jnp.bfloat16)
        lagged = jnp.einsum('krab,krl->lab', cross_spec.astype(jnp.float32), inverse)
        return lagged.astype(jnp.bfloat16)
    flattened = lax.map(one_slot, (pair_table.reshape(N_BAND * PCAP, 4), live_slots.reshape(N_BAND * PCAP)))
    return flattened.reshape(N_BAND, PCAP, L, BLK, BLK)
```

```python
import functools
import math

import jax
import jax.numpy as jnp
import numpy as np
from jax import lax
from jax.experimental import pallas as pl
from jax.experimental.pallas import tpu as pltpu
from jax.sharding import PartitionSpec as P

BLK = 128
SUB = 64
EPSILON = 1e-06
QUAD = 4
PAD = 136
BF = jnp.bfloat16


def forward_table(samples):
    n = np.arange(samples)[None, :]
    k = np.arange(samples // 2)[:, None]
    angles = (n * k % samples) * (2.0 * math.pi / samples)
    factor = 1.0 / math.sqrt(samples)
    table = np.concatenate([np.cos(angles) * factor, -np.sin(angles) * factor], axis=0)
    return jnp.asarray(table.astype(np.float32), dtype=BF)


def inverse_table(samples):
    k = np.arange(samples // 2)[None, :]
    t = np.arange(samples)[:, None]
    angles = (t * k % samples) * (2.0 * math.pi / samples)
    factor = 2.0 / math.sqrt(samples // 2)
    table = np.stack([np.cos(angles) * factor, -np.sin(angles) * factor], axis=2)
    return jnp.asarray(table.reshape(samples, samples).astype(np.float32), dtype=BF)


def whiten_kernel(strain_ref, table_ref, out_ref, rows_ref):
    segments, channels, samples = strain_ref.shape
    bins = samples // 2
    for g in range(channels // BLK):
        for s in range(segments):
            x = strain_ref[s, g * BLK : (g + 1) * BLK, :]
            spec = lax.dot_general(
                table_ref[...], x, (((1,), (1,)), ((), ())), preferred_element_type=jnp.float32
            )
            re, im = spec[:bins], spec[bins:]
            power = re * re + im * im
            for m in range(bins // SUB):
                cut = slice(m * SUB, (m + 1) * SUB)
                level = jnp.mean(power[cut], axis=0, keepdims=True)
                scale = 1.0 / jnp.sqrt(level + EPSILON)
                for r, part in enumerate((re, im)):
                    rows_ref[r, pl.ds(m * SUB * segments + s, SUB, stride=segments), :] = (
                        part[cut] * scale
                    )
        for r in range(2):
            out_ref[g, :, r] = rows_ref[r].reshape(bins // QUAD, QUAD * segments, BLK).astype(BF)


def whiten(strain_rate):
    segments, channels, samples = strain_rate.shape
    bins = samples // 2
    return pl.pallas_call(
        whiten_kernel,
        out_shape=jax.ShapeDtypeStruct(
            (channels // BLK, bins // QUAD, 2, QUAD * segments, BLK), BF
        ),
        in_specs=[pl.BlockSpec(memory_space=pltpu.VMEM)] * 2,
        out_specs=pl.BlockSpec(memory_space=pltpu.VMEM),
        scratch_shapes=[pltpu.VMEM((2, bins * segments, BLK), jnp.float32)],
    )(strain_rate, forward_table(samples))


def cross_quad(left, right, factors, planes_ref, first):
    depth = left.shape[0] * left.shape[1] * left.shape[2]
    left_t = left.reshape(depth, BLK).T
    bin_of = lax.broadcasted_iota(jnp.int32, left_t.shape, 1) % 16 // 4
    stacked = jnp.concatenate(
        [jnp.where(bin_of == q, left_t, jnp.zeros_like(left_t)) for q in range(QUAD)], axis=0
    )
    turned = jnp.stack([-right[:, 1], right[:, 0]], axis=1)
    both = jnp.concatenate([right.reshape(depth, BLK), turned.reshape(depth, BLK)], axis=1)
    product = jnp.dot(stacked, both, preferred_element_type=jnp.float32)
    for q in range(QUAD):
        for r in range(2):
            planes_ref[pl.ds((first + q * 2 + r) * PAD, BLK), :] = (
                product[q * BLK : (q + 1) * BLK, r * BLK : (r + 1) * BLK] * factors[q]
            )


def bin_factors(pair_ref, first_bin, segments):
    lo, hi, live = pair_ref[2], pair_ref[3], pair_ref[4]
    return [
        jnp.where(
            (lo <= first_bin + q) & (first_bin + q < hi) & (live > 0), 1.0 / segments, 0.0
        ).astype(jnp.float32)
        for q in range(QUAD)
    ]


def cross_kernel(pair_ref, blocks_ref, out_ref, planes_ref):
    segments = blocks_ref.shape[0] * blocks_ref.shape[4] // QUAD
    groups = blocks_ref.shape[2]
    for g in range(groups):
        first_bin = (pl.program_id(0) * groups + g) * QUAD
        cross_quad(
            blocks_ref[:, 0, g],
            blocks_ref[:, 1, g],
            bin_factors(pair_ref, first_bin, segments),
            planes_ref,
            g * QUAD * 2,
        )
    for a in range(BLK):
        out_ref[a] = planes_ref[pl.ds(a, groups * QUAD * 2, stride=PAD), :].astype(BF)


def cross(pair, blocks):
    sources, _, quads, _, rows, _ = blocks.shape
    groups = 2
    return pl.pallas_call(
        cross_kernel,
        grid=(quads // groups,),
        out_shape=jax.ShapeDtypeStruct((BLK, quads * QUAD * 2, BLK), BF),
        in_specs=[
            pl.BlockSpec(memory_space=pltpu.SMEM),
            pl.BlockSpec((sources, 2, groups, 2, rows, BLK), lambda c: (0, 0, c, 0, 0, 0)),
        ],
        out_specs=pl.BlockSpec((BLK, groups * QUAD * 2, BLK), lambda c: (0, c, 0)),
        scratch_shapes=[pltpu.VMEM((groups * QUAD * 2 * PAD, BLK), jnp.float32)],
    )(pair, blocks)


def lag_kernel(table_ref, cross_ref, out_ref, rows_ref):
    lags, depth = table_ref.shape
    width = cross_ref.shape[0]
    wide = rows_ref.shape[0] // lags
    for a in range(0, width, 2):
        both = jnp.concatenate([cross_ref[a], cross_ref[a + 1]], axis=1)
        lagged = jnp.dot(table_ref[...], both, preferred_element_type=jnp.float32)
        for d in range(2):
            rows_ref[pl.ds(a + d, lags, stride=wide), :] = lagged[:, d * BLK : (d + 1) * BLK]
    out_ref[...] = rows_ref[...].reshape(lags, wide, BLK)[:, :width].astype(BF)


def lag(cross_spec):
    channels, depth, _ = cross_spec.shape
    lags, width = depth, 16
    return pl.pallas_call(
        lag_kernel,
        grid=(channels // width,),
        out_shape=jax.ShapeDtypeStruct((lags, channels, BLK), BF),
        in_specs=[
            pl.BlockSpec((lags, depth), lambda a: (0, 0)),
            pl.BlockSpec((width, depth, BLK), lambda a: (a, 0, 0)),
        ],
        out_specs=pl.BlockSpec((lags, width, BLK), lambda a: (0, a, 0)),
        scratch_shapes=[pltpu.VMEM((lags * (width + 8), BLK), jnp.float32)],
        compiler_params=pltpu.CompilerParams(vmem_limit_bytes=48 << 20),
    )(inverse_table(lags), cross_spec)


def body(strain_rate, pair_table, pair_count):
    whitened = whiten(strain_rate)
    gathered = lax.all_gather(whitened, "band", axis=0, tiled=True)
    band, tm = lax.axis_index("band"), lax.axis_index("tm")
    pairs = lax.dynamic_index_in_dim(pair_table, band, 0, keepdims=False)
    live = (tm < lax.dynamic_index_in_dim(pair_count, band, 0, keepdims=False)).astype(jnp.int32)
    mine = jnp.concatenate([lax.dynamic_index_in_dim(pairs, tm, 0, keepdims=False), live[None]])
    chosen = jnp.take(gathered, pairs[:, :2].reshape(-1), axis=0)
    chosen = chosen.reshape((pairs.shape[0], 2) + whitened.shape[1:])
    blocks = lax.all_to_all(chosen, "tm", split_axis=0, concat_axis=0, tiled=True)
    return lag(cross(mine, blocks))[None, None]


def solution(mesh):
    return jax.shard_map(
        body,
        mesh=mesh,
        in_specs=(P("tm", "band", None), P(), P()),
        out_specs=P("band", "tm", None, None, None),
        check_vma=False,
    )
```

```python
import math

import jax
import jax.numpy as jnp
import numpy as np
from jax import lax
from jax.experimental import pallas as pl
from jax.experimental.pallas import tpu as pltpu
from jax.sharding import PartitionSpec as P

BLK = 128
SUB = 64
EPSILON = 1e-06
MESH = pl.DeviceIdType.MESH
SIDE = 4
QUAD = 4
GROUPS = 1
STAGE = (0, 2, 4, 6, 8)
PAD = 136
BF = jnp.bfloat16


def forward_table(samples):
    n = np.arange(samples)[None, :]
    k = np.arange(samples // 2)[:, None]
    angles = (n * k % samples) * (2.0 * math.pi / samples)
    factor = 1.0 / math.sqrt(samples)
    table = np.concatenate([np.cos(angles) * factor, -np.sin(angles) * factor], axis=0)
    return jnp.asarray(table.astype(np.float32), dtype=BF)


def inverse_table(samples):
    k = np.arange(samples // 2)[None, :]
    t = np.arange(samples)[:, None]
    angles = (t * k % samples) * (2.0 * math.pi / samples)
    factor = 2.0 / math.sqrt(samples // 2)
    table = np.stack([np.cos(angles) * factor, -np.sin(angles) * factor], axis=2)
    return jnp.asarray(table.reshape(samples, samples).astype(np.float32), dtype=BF)


def whiten_kernel(strain_ref, table_ref, out_ref, rows_ref):
    chunks, _, groups = out_ref.shape[:3]
    segments, channels, samples = strain_ref.shape
    bins = samples // 2
    for g in range(channels // BLK):
        for s in range(segments):
            x = strain_ref[s, g * BLK : (g + 1) * BLK, :]
            spec = lax.dot_general(
                table_ref[...], x, (((1,), (1,)), ((), ())), preferred_element_type=jnp.float32
            )
            re, im = spec[:bins], spec[bins:]
            power = re * re + im * im
            for m in range(bins // SUB):
                cut = slice(m * SUB, (m + 1) * SUB)
                level = jnp.mean(power[cut], axis=0, keepdims=True)
                scale = 1.0 / jnp.sqrt(level + EPSILON)
                for r, part in enumerate((re, im)):
                    rows_ref[r, pl.ds(m * SUB * segments + s, SUB, stride=segments), :] = (
                        part[cut] * scale
                    )
        for r in range(2):
            tiles = rows_ref[r].reshape(chunks, groups, QUAD * segments, BLK)
            out_ref[:, g, :, r] = tiles.astype(BF)


def whiten(strain_rate):
    segments, channels, samples = strain_rate.shape
    bins = samples // 2
    return pl.pallas_call(
        whiten_kernel,
        out_shape=jax.ShapeDtypeStruct(
            (bins // QUAD // GROUPS, channels // BLK, GROUPS, 2, QUAD * segments, BLK), BF
        ),
        in_specs=[pl.BlockSpec(memory_space=pltpu.VMEM)] * 2,
        out_specs=pl.BlockSpec(memory_space=pltpu.VMEM),
        scratch_shapes=[pltpu.VMEM((2, bins * segments, BLK), jnp.float32)],
    )(strain_rate, forward_table(samples))


def cross_quad(left, right, factors, planes_ref, first):
    depth = left.shape[0] * left.shape[1] * left.shape[2]
    left_t = left.reshape(depth, BLK).T
    bin_of = lax.broadcasted_iota(jnp.int32, left_t.shape, 1) % 16 // 4
    stacked = jnp.concatenate(
        [jnp.where(bin_of == q, left_t, jnp.zeros_like(left_t)) for q in range(QUAD)], axis=0
    )
    turned = jnp.stack([-right[:, 1], right[:, 0]], axis=1)
    both = jnp.concatenate([right.reshape(depth, BLK), turned.reshape(depth, BLK)], axis=1)
    product = jnp.dot(stacked, both, preferred_element_type=jnp.float32)
    for q in range(QUAD):
        for r in range(2):
            planes_ref[pl.ds((first + q * 2 + r) * PAD, BLK), :] = (
                product[q * BLK : (q + 1) * BLK, r * BLK : (r + 1) * BLK] * factors[q]
            )


def bin_factors(pair_ref, slot, first_bin, segments):
    lo, hi, live = pair_ref[slot, 2], pair_ref[slot, 3], pair_ref[slot, 4]
    return [
        jnp.where(
            (lo <= first_bin + q) & (first_bin + q < hi) & (live > 0), 1.0 / segments, 0.0
        ).astype(jnp.float32)
        for q in range(QUAD)
    ]


def move_kernel(
    pair_ref, own_ref, out_ref, gat, pick, stage, got, planes, tiles, send, recv, out_sem
):
    chunks = own_ref.shape[0]
    ticks = chunks // 2
    tm, band = lax.axis_index("tm"), lax.axis_index("band")
    y, core, x, z = tm // 2, tm % 2, band // SIDE, band % SIDE
    across = [(1, 0), (3, 0), (2, 0), (1, 1), (3, 1), (2, 1), (0, 1)]

    def along(axis, step):
        if axis == 0:
            return (tm, lax.rem(x + step, SIDE) * SIDE + z)
        return (tm, x * SIDE + lax.rem(z + step, SIDE))

    def over(dy, dc, sign=1):
        return lax.rem(y + SIDE + sign * dy, SIDE) * 2 + lax.rem(core + dc, 2)

    def block_at(c, axis, step):
        if axis == 0:
            return gat.at[c, lax.rem(x + step, SIDE), z]
        return gat.at[c, x, lax.rem(z + step, SIDE)]

    def line_at(c, axis, step, first, count):
        if axis == 0:
            return gat.at[c, lax.rem(x + step, SIDE), pl.ds(first, count)]
        return gat.at[c, pl.ds(first, count), lax.rem(z + step, SIDE)]

    def copy(src, dst, c, slot, device):
        return pltpu.make_async_remote_copy(
            src_ref=src,
            dst_ref=dst,
            send_sem=send.at[c, slot],
            recv_sem=recv.at[c, slot],
            device_id=device,
            device_id_type=MESH,
        )

    def first(c, axis):
        out = [
            (own_ref.at[c], block_at(c, axis, 0), c, k, along(axis, d))
            for k, d in enumerate((1, 3, 2))
        ]
        into = [
            (own_ref.at[c], block_at(c, axis, SIDE - d), c, k, along(axis, d))
            for k, d in enumerate((1, 3, 2))
        ]
        return out, into

    def second(c, axis):
        out, into = [], []
        for k, d in ((3, 1), (4, 3)):
            mine = line_at(c, axis, 0, 0, SIDE)
            out.append((mine, mine, c, k, along(axis, d)))
            theirs = line_at(c, axis, SIDE - d, 0, SIDE)
            into.append((theirs, theirs, c, k, along(axis, d)))
        return out, into

    def third(c, axis):
        out, into = [], []
        half = SIDE // 2
        for k, d, at in ((5, 1, 0), (6, 3, half)):
            passed = line_at(c, axis, SIDE - d, at, half)
            out.append((passed, passed, c, k, along(axis, d)))
            theirs = line_at(c, axis, 2, at, half)
            into.append((theirs, theirs, c, k, along(axis, d)))
        return out, into

    def last(c):
        out, into = [], []
        for k, (dy, dc) in enumerate(across):
            to, source = over(dy, dc), over(dy, dc, -1)
            out.append((stage.at[c, to], got.at[c, tm], c, 7 + k, (to, band)))
            into.append((stage.at[c, to], got.at[c, source], c, 7 + k, (to, band)))
        return out, into

    def starts(copies):
        for one in copies:
            copy(*one).start()

    def arrivals(copies):
        for one in copies:
            copy(*one).wait_recv()

    def departures(copies):
        for one in copies:
            copy(*one).wait_send()

    def select(c):
        shape = pick.shape
        pick[...] = gat[c].reshape(shape)
        for p in range(stage.shape[1]):
            for w in range(2):
                stage[c, p, w] = pick[pair_ref[p, w]]
        for w in range(2):
            got[c, tm, w] = pick[pair_ref[tm, w]]

    def write(u, slot):
        rows = tiles.shape[2]
        return pltpu.make_async_copy(
            tiles.at[slot], out_ref.at[:, pl.ds(u * rows, rows), :], out_sem.at[slot]
        )

    def compute(u):
        groups = got.shape[3]
        segments = got.shape[1] * got.shape[5] // QUAD
        for h in range(2):
            c = 2 * u + h
            for g in range(groups):
                factors = bin_factors(pair_ref, tm, (c * groups + g) * QUAD, segments)
                cross_quad(
                    got[c, :, 0, g], got[c, :, 1, g], factors, planes, (h * groups + g) * QUAD * 2
                )
        slot = lax.rem(u, 2)

        @pl.when(u >= 2)
        def _():
            write(u - 2, slot).wait()

        rows = tiles.shape[2]
        for a in range(BLK):
            tiles[slot, a] = planes[pl.ds(a, rows, stride=PAD), :].astype(BF)
        write(u, slot).start()

    barrier = pltpu.get_barrier_semaphore()
    partners = [along(axis, d) for axis in (0, 1) for d in (1, 2, 3)]
    partners += [(over(dy, dc), band) for dy, dc in across]
    for partner in partners:
        pl.semaphore_signal(barrier, inc=1, device_id=partner, device_id_type=MESH)
    pl.semaphore_wait(barrier, len(partners))

    def tick(u, _):
        def at(lag, act):
            v = u - lag

            @pl.when((v >= 0) & (v < ticks))
            def _():
                act(v)

        def both(act):
            def run(v):
                for h in range(2):
                    act(2 * v + h, h)

            return run

        def begin(c, h):
            gat[c, x, z] = own_ref[c]
            starts(first(c, h)[0])

        def spread(c, h):
            arrivals(first(c, h)[1])
            starts(second(c, 1 - h)[0])

        def relay(c, h):
            arrivals(second(c, 1 - h)[1])
            starts(third(c, 1 - h)[0])

        def cross_over(c, h):
            arrivals(third(c, 1 - h)[1])
            select(c)
            starts(last(c)[0])

        def finish(v):
            for h in range(2):
                c = 2 * v + h
                arrivals(last(c)[1])
                departures(first(c, h)[0])
                departures(second(c, 1 - h)[0])
                departures(third(c, 1 - h)[0])
                departures(last(c)[0])
            compute(v)

        at(STAGE[0], both(begin))
        at(STAGE[1], both(spread))
        at(STAGE[2], both(relay))
        at(STAGE[3], both(cross_over))
        at(STAGE[4], finish)
        return 0

    lax.fori_loop(0, ticks + STAGE[4], tick, 0)
    for u in range(ticks - 2, ticks):
        write(u, u % 2).wait()


def move(pairs, own):
    chunks, blocks, groups, parts, rows, _ = own.shape
    bands, slots = SIDE * SIDE, pairs.shape[0]
    tail = (groups, parts, rows, BLK)
    planes = 2 * groups * QUAD * parts
    depth = chunks * groups * QUAD * parts
    return pl.pallas_call(
        move_kernel,
        out_shape=jax.ShapeDtypeStruct((BLK, depth, BLK), BF),
        in_specs=[
            pl.BlockSpec(memory_space=pltpu.SMEM),
            pl.BlockSpec(memory_space=pltpu.VMEM),
        ],
        out_specs=pl.BlockSpec(memory_space=pl.ANY),
        scratch_shapes=[
            pltpu.VMEM((chunks, SIDE, SIDE, blocks) + tail, BF),
            pltpu.VMEM((bands * blocks,) + tail, BF),
            pltpu.VMEM((chunks, slots, 2) + tail, BF),
            pltpu.VMEM((chunks, slots, 2) + tail, BF),
            pltpu.VMEM((planes * PAD, BLK), jnp.float32),
            pltpu.VMEM((2, BLK, planes, BLK), BF),
            pltpu.SemaphoreType.DMA((chunks, 14)),
            pltpu.SemaphoreType.DMA((chunks, 14)),
            pltpu.SemaphoreType.DMA((2,)),
        ],
        compiler_params=pltpu.CompilerParams(
            collective_id=0, has_side_effects=True, vmem_limit_bytes=48 << 20
        ),
    )(pairs, own)


def lag_kernel(table_ref, cross_ref, out_ref, rows_ref):
    lags, depth = table_ref.shape
    width = cross_ref.shape[0]
    wide = rows_ref.shape[0] // lags
    for a in range(0, width, 2):
        both = jnp.concatenate([cross_ref[a], cross_ref[a + 1]], axis=1)
        lagged = jnp.dot(table_ref[...], both, preferred_element_type=jnp.float32)
        for d in range(2):
            rows_ref[pl.ds(a + d, lags, stride=wide), :] = lagged[:, d * BLK : (d + 1) * BLK]
    out_ref[...] = rows_ref[...].reshape(lags, wide, BLK)[:, :width].astype(BF)


def lag(cross_spec):
    channels, depth, _ = cross_spec.shape
    lags, width = depth, 16
    return pl.pallas_call(
        lag_kernel,
        grid=(channels // width,),
        out_shape=jax.ShapeDtypeStruct((lags, channels, BLK), BF),
        in_specs=[
            pl.BlockSpec((lags, depth), lambda a: (0, 0)),
            pl.BlockSpec((width, depth, BLK), lambda a: (a, 0, 0)),
        ],
        out_specs=pl.BlockSpec((lags, width, BLK), lambda a: (0, a, 0)),
        scratch_shapes=[pltpu.VMEM((lags * (width + 8), BLK), jnp.float32)],
        compiler_params=pltpu.CompilerParams(vmem_limit_bytes=48 << 20),
    )(inverse_table(lags), cross_spec)


def body(strain_rate, pair_table, pair_count):
    whitened = whiten(strain_rate)
    band = lax.axis_index("band")
    pairs = lax.dynamic_index_in_dim(pair_table, band, 0, keepdims=False)
    count = lax.dynamic_index_in_dim(pair_count, band, 0, keepdims=False)
    live = jnp.arange(pairs.shape[0], dtype=jnp.int32) < count
    pairs = jnp.concatenate([pairs, live[:, None].astype(jnp.int32)], axis=1)
    return lag(move(pairs, whitened))[None, None]


def solution(mesh):
    return jax.shard_map(
        body,
        mesh=mesh,
        in_specs=(P("tm", "band", None), P(), P()),
        out_specs=P("band", "tm", None, None, None),
        check_vma=False,
    )
```

```python
import math

import jax
import jax.numpy as jnp
import numpy as np
from jax import lax
from jax.experimental import pallas as pl
from jax.experimental.pallas import tpu as pltpu
from jax.sharding import PartitionSpec as P

BLK = 128
SUB = 64
EPSILON = 1e-06
MESH = pl.DeviceIdType.MESH
SIDE = 4
QUAD = 4
PAD = 136
BF = jnp.bfloat16


def forward_table(samples):
    n = np.arange(samples)[None, :]
    k = np.arange(samples // 2)[:, None]
    angles = (n * k % samples) * (2.0 * math.pi / samples)
    factor = 1.0 / math.sqrt(samples)
    table = np.concatenate([np.cos(angles) * factor, -np.sin(angles) * factor], axis=0)
    return jnp.asarray(table.astype(np.float32), dtype=BF)


def inverse_table(samples):
    k = np.arange(samples // 2)[None, :]
    t = np.arange(samples)[:, None]
    angles = (t * k % samples) * (2.0 * math.pi / samples)
    factor = 2.0 / math.sqrt(samples // 2)
    table = np.stack([np.cos(angles) * factor, -np.sin(angles) * factor], axis=2)
    return jnp.asarray(table.reshape(samples, samples).astype(np.float32), dtype=BF)


def whiten_kernel(strain_ref, table_ref, out_ref, rows_ref):
    chunks, groups = out_ref.shape[:2]
    segments, channels, samples = strain_ref.shape
    bins = samples // 2
    for g in range(channels // BLK):
        for s in range(segments):
            x = strain_ref[s, g * BLK : (g + 1) * BLK, :]
            spec = lax.dot_general(
                table_ref[...], x, (((1,), (1,)), ((), ())), preferred_element_type=jnp.float32
            )
            re, im = spec[:bins], spec[bins:]
            power = re * re + im * im
            for m in range(bins // SUB):
                cut = slice(m * SUB, (m + 1) * SUB)
                level = jnp.mean(power[cut], axis=0, keepdims=True)
                scale = 1.0 / jnp.sqrt(level + EPSILON)
                for r, part in enumerate((re, im)):
                    rows_ref[r, pl.ds(m * SUB * segments + s, SUB, stride=segments), :] = (
                        part[cut] * scale
                    )
        for r in range(2):
            tiles = rows_ref[r].reshape(chunks, groups, QUAD * segments, BLK)
            out_ref[:, :, g, r] = tiles.astype(BF)


def whiten(strain_rate):
    segments, channels, samples = strain_rate.shape
    bins = samples // 2
    return pl.pallas_call(
        whiten_kernel,
        out_shape=jax.ShapeDtypeStruct(
            (bins // QUAD // SIDE, SIDE, channels // BLK, 2, QUAD * segments, BLK), BF
        ),
        in_specs=[pl.BlockSpec(memory_space=pltpu.VMEM)] * 2,
        out_specs=pl.BlockSpec(memory_space=pltpu.VMEM),
        scratch_shapes=[pltpu.VMEM((2, bins * segments, BLK), jnp.float32)],
    )(strain_rate, forward_table(samples))


def cross_quad(left, right, factors, planes_ref, first):
    depth = left.shape[0] * left.shape[1] * left.shape[2]
    left_t = left.reshape(depth, BLK).T
    bin_of = lax.broadcasted_iota(jnp.int32, left_t.shape, 1) % 16 // 4
    stacked = jnp.concatenate(
        [jnp.where(bin_of == q, left_t, jnp.zeros_like(left_t)) for q in range(QUAD)], axis=0
    )
    turned = jnp.stack([-right[:, 1], right[:, 0]], axis=1)
    both = jnp.concatenate([right.reshape(depth, BLK), turned.reshape(depth, BLK)], axis=1)
    product = jnp.dot(stacked, both, preferred_element_type=jnp.float32)
    for q in range(QUAD):
        for r in range(2):
            planes_ref[pl.ds((first + q * 2 + r) * PAD, BLK), :] = (
                product[q * BLK : (q + 1) * BLK, r * BLK : (r + 1) * BLK] * factors[q]
            )


def bin_factors(pair_ref, band, slot, first_bin, segments):
    lo, hi = pair_ref[band, slot * 4 + 2], pair_ref[band, slot * 4 + 3]
    live = slot < pair_ref[band, 32]
    return [
        jnp.where(
            (lo <= first_bin + q) & (first_bin + q < hi) & live, 1.0 / segments, 0.0
        ).astype(jnp.float32)
        for q in range(QUAD)
    ]


def move_kernel(
    pair_ref, own_ref, out_ref, gat, pick, stage, got, planes, tiles, send, recv, out_sem
):
    chunks = own_ref.shape[0]
    ticks = chunks // 2
    tm, band = lax.axis_index("tm"), lax.axis_index("band")
    y, core, x, z = tm // 2, tm % 2, band // SIDE, band % SIDE
    steps = (1, 3, 2)
    moves = [(dv, dy, dc) for dc in (0, 1) for dv in range(SIDE) for dy in range(SIDE)]
    moves = [moves[(11 * k) % len(moves)] for k in range(len(moves))]
    moves = [m for m in moves if m != (0, 0, 0)]

    def around(at, step):
        return lax.rem(at + step, SIDE)

    def on_line(h, place):
        return x * SIDE + place if h == 0 else place * SIDE + z

    def on_cross(h, place):
        return place * SIDE + z if h == 0 else x * SIDE + place

    def mine(h):
        return (z, x) if h == 0 else (x, z)

    def copy(src, dst, c, slot, device):
        return pltpu.make_async_remote_copy(
            src_ref=src,
            dst_ref=dst,
            send_sem=send.at[c, slot],
            recv_sem=recv.at[c, slot],
            device_id=device,
            device_id_type=MESH,
        )

    def scatter(c, h):
        out, into = [], []
        v = mine(h)[0]
        for k, d in enumerate(steps):
            to, source = around(v, d), around(v, SIDE - d)
            there = gat.at[c, x, source] if h == 0 else gat.at[c, source, z]
            device = (tm, on_line(h, to))
            out.append((own_ref.at[c, to], gat.at[c, x, z], c, k, device))
            into.append((own_ref.at[c, to], there, c, k, device))
        return out, into

    def gather(c, h):
        out, into = [], []
        w = mine(h)[1]
        for k, d in enumerate(steps):
            here = gat.at[c, x] if h == 0 else gat.at[c, :, z]
            source = around(w, SIDE - d)
            there = gat.at[c, source] if h == 0 else gat.at[c, :, source]
            device = (tm, on_cross(h, around(w, d)))
            out.append((here, here, c, 3 + k, device))
            into.append((there, there, c, 3 + k, device))
        return out, into

    def deal(c, h):
        out, into = [], []
        v = mine(h)[0]
        for k, (dv, dy, dc) in enumerate(moves):
            to_v, to_t = around(v, dv), around(y, dy) * 2 + lax.rem(core + dc, 2)
            from_v = around(v, SIDE - dv)
            from_t = around(y, SIDE - dy) * 2 + lax.rem(core + dc, 2)
            src, device = stage.at[c, to_v, to_t], (to_t, on_line(h, to_v))
            out.append((src, got.at[c, v, tm], c, 6 + k, device))
            into.append((src, got.at[c, from_v, from_t], c, 6 + k, device))
        return out, into

    def starts(*lists):
        for group in zip(*lists):
            for one in group:
                copy(*one).start()

    def arrivals(copies):
        for one in copies:
            copy(*one).wait_recv()

    def departures(copies):
        for one in copies:
            copy(*one).wait_send()

    def select(c, h):
        pick[...] = gat[c].reshape(pick.shape)
        for v in range(SIDE):
            owner = on_line(h, v)
            for p in range(stage.shape[2]):
                for w in range(2):
                    stage[c, v, p, w] = pick[pair_ref[owner, p * 4 + w]]
        for w in range(2):
            got[c, mine(h)[0], tm, w] = pick[pair_ref[band, tm * 4 + w]]

    def write(c, slot):
        rows = tiles.shape[2]
        return pltpu.make_async_copy(
            tiles.at[slot], out_ref.at[:, pl.ds(c * rows, rows), :], out_sem.at[slot]
        )

    def compute(c, slot):
        segments = got.shape[2] * got.shape[5] // QUAD
        for g in range(SIDE):
            factors = bin_factors(pair_ref, band, tm, (c * SIDE + g) * QUAD, segments)
            cross_quad(got[c, g, :, 0], got[c, g, :, 1], factors, planes, g * QUAD * 2)

        @pl.when(c >= 2)
        def _():
            write(c - 2, slot).wait()

        rows = tiles.shape[2]
        for a in range(BLK):
            tiles[slot, a] = planes[pl.ds(a, rows, stride=PAD), :].astype(BF)
        write(c, slot).start()

    barrier = pltpu.get_barrier_semaphore()
    partners = [(tm, on_cross(0, around(x, d))) for d in steps]
    partners += [(tm, on_cross(1, around(z, d))) for d in steps]
    for h in range(2):
        for dv, dy, dc in moves:
            if dv or h == 0:
                if (dv, dy, dc) not in ((1, 0, 0), (2, 0, 0), (3, 0, 0)):
                    to_t = around(y, dy) * 2 + lax.rem(core + dc, 2)
                    partners.append((to_t, on_line(h, around(mine(h)[0], dv))))
    for partner in partners:
        pl.semaphore_signal(barrier, inc=1, device_id=partner, device_id_type=MESH)
    pl.semaphore_wait(barrier, len(partners))

    def spread(u):
        for h in range(2):
            arrivals(scatter(2 * u + h, h)[1])
        starts(*[gather(2 * u + h, h)[0] for h in range(2)])

    def begin(u, _):
        for h in range(2):
            c = 2 * u + h
            gat[c, x, z] = own_ref[c, mine(h)[0]]
        starts(*[scatter(2 * u + h, h)[0] for h in range(2)])
        return 0

    def tick(u, _):
        @pl.when(u + 1 < ticks)
        def _():
            spread(u + 1)

        @pl.when(u < ticks)
        def _():
            for h in range(2):
                arrivals(gather(2 * u + h, h)[1])
                select(2 * u + h, h)
            starts(*[deal(2 * u + h, h)[0] for h in range(2)])

        @pl.when(u >= 1)
        def _():
            for h in range(2):
                c = 2 * (u - 1) + h
                arrivals(deal(c, h)[1])
                compute(c, h)
            for h in range(2):
                c = 2 * (u - 1) + h
                departures(scatter(c, h)[0])
                departures(gather(c, h)[0])
                departures(deal(c, h)[0])

        return 0

    lax.fori_loop(0, ticks, begin, 0)
    spread(0)
    lax.fori_loop(0, ticks + 1, tick, 0)
    for h in range(2):
        write(chunks - 2 + h, h).wait()


def move(pairs, own):
    chunks, groups, blocks, parts, rows, _ = own.shape
    bands, slots = SIDE * SIDE, 2 * SIDE
    tail = (parts, rows, BLK)
    planes = groups * QUAD * parts
    depth = chunks * planes
    return pl.pallas_call(
        move_kernel,
        out_shape=jax.ShapeDtypeStruct((BLK, depth, BLK), BF),
        in_specs=[
            pl.BlockSpec(memory_space=pltpu.SMEM),
            pl.BlockSpec(memory_space=pltpu.VMEM),
        ],
        out_specs=pl.BlockSpec(memory_space=pl.ANY),
        scratch_shapes=[
            pltpu.VMEM((chunks, SIDE, SIDE, blocks) + tail, BF),
            pltpu.VMEM((bands * blocks,) + tail, BF),
            pltpu.VMEM((chunks, SIDE, slots, 2) + tail, BF),
            pltpu.VMEM((chunks, groups, slots, 2) + tail, BF),
            pltpu.VMEM((planes * PAD, BLK), jnp.float32),
            pltpu.VMEM((2, BLK, planes, BLK), BF),
            pltpu.SemaphoreType.DMA((chunks, 37)),
            pltpu.SemaphoreType.DMA((chunks, 37)),
            pltpu.SemaphoreType.DMA((2,)),
        ],
        compiler_params=pltpu.CompilerParams(
            collective_id=0, has_side_effects=True, vmem_limit_bytes=24 << 20
        ),
    )(pairs, own)


def lag_kernel(table_ref, cross_ref, out_ref, rows_ref):
    lags, depth = table_ref.shape
    width = cross_ref.shape[0]
    wide = rows_ref.shape[0] // lags
    for a in range(0, width, 2):
        both = jnp.concatenate([cross_ref[a], cross_ref[a + 1]], axis=1)
        lagged = jnp.dot(table_ref[...], both, preferred_element_type=jnp.float32)
        for d in range(2):
            rows_ref[pl.ds(a + d, lags, stride=wide), :] = lagged[:, d * BLK : (d + 1) * BLK]
    out_ref[...] = rows_ref[...].reshape(lags, wide, BLK)[:, :width].astype(BF)


def lag(cross_spec):
    channels, depth, _ = cross_spec.shape
    lags, width = depth, 16
    return pl.pallas_call(
        lag_kernel,
        grid=(channels // width,),
        out_shape=jax.ShapeDtypeStruct((lags, channels, BLK), BF),
        in_specs=[
            pl.BlockSpec((lags, depth), lambda a: (0, 0)),
            pl.BlockSpec((width, depth, BLK), lambda a: (a, 0, 0)),
        ],
        out_specs=pl.BlockSpec((lags, width, BLK), lambda a: (0, a, 0)),
        scratch_shapes=[pltpu.VMEM((lags * (width + 8), BLK), jnp.float32)],
        compiler_params=pltpu.CompilerParams(vmem_limit_bytes=24 << 20),
    )(inverse_table(lags), cross_spec)


def body(strain_rate, pair_table, pair_count):
    whitened = whiten(strain_rate)
    pairs = jnp.concatenate([pair_table.reshape(pair_table.shape[0], -1), pair_count[:, None]], axis=1)
    return lag(move(pairs, whitened))[None, None]


def solution(mesh):
    return jax.shard_map(
        body,
        mesh=mesh,
        in_specs=(P("tm", "band", None), P(), P()),
        out_specs=P("band", "tm", None, None, None),
        check_vma=False,
    )
```

```python
import math

import jax
import jax.numpy as jnp
import numpy as np
from jax import lax
from jax.experimental import pallas as pl
from jax.experimental.pallas import tpu as pltpu
from jax.sharding import PartitionSpec as P

BLK = 128
SUB = 64
EPSILON = 1e-06
MESH = pl.DeviceIdType.MESH
SIDE = 4
QUAD = 4
PAD = 136
BF = jnp.bfloat16


def forward_table(samples):
    n = np.arange(samples)[None, :]
    k = np.arange(samples // 2)[:, None]
    angles = (n * k % samples) * (2.0 * math.pi / samples)
    factor = 1.0 / math.sqrt(samples)
    table = np.concatenate([np.cos(angles) * factor, -np.sin(angles) * factor], axis=0)
    return jnp.asarray(table.astype(np.float32), dtype=BF)


def inverse_table(samples):
    k = np.arange(samples // 2)[None, :]
    t = np.arange(samples)[:, None]
    angles = (t * k % samples) * (2.0 * math.pi / samples)
    factor = 2.0 / math.sqrt(samples // 2)
    table = np.stack([np.cos(angles) * factor, -np.sin(angles) * factor], axis=2)
    return jnp.asarray(table.reshape(samples, samples).astype(np.float32), dtype=BF)


def whiten(strain_ref, table_ref, own, own_late, rows_ref):
    segments, channels, samples = strain_ref.shape
    bins = samples // 2
    chunks, groups = own.shape[:2]
    early = chunks * groups
    for g in range(channels // BLK):
        for s in range(segments):
            x = strain_ref[s, g * BLK : (g + 1) * BLK, :]
            spec = lax.dot_general(
                table_ref[...], x, (((1,), (1,)), ((), ())), preferred_element_type=jnp.float32
            )
            re, im = spec[:bins], spec[bins:]
            power = re * re + im * im
            for m in range(bins // SUB):
                cut = slice(m * SUB, (m + 1) * SUB)
                level = jnp.mean(power[cut], axis=0, keepdims=True)
                scale = 1.0 / jnp.sqrt(level + EPSILON)
                for r, part in enumerate((re, im)):
                    rows_ref[r, pl.ds(m * SUB * segments + s, SUB, stride=segments), :] = (
                        part[cut] * scale
                    )
        for r in range(2):
            tiles = rows_ref[r].reshape(bins // QUAD, QUAD * segments, BLK).astype(BF)
            own[:, :, g, r] = tiles[:early].reshape(chunks, groups, QUAD * segments, BLK)
            for k in range(early, bins // QUAD):
                own_late[(k - early) * 2 + r, g] = tiles[k]


def cross_quad(left, right, turned, factors, planes_ref, first):
    left_t = left.T
    bin_of = lax.broadcasted_iota(jnp.int32, left_t.shape, 1) % 16 // 4
    stacked = jnp.concatenate(
        [jnp.where(bin_of == q, left_t, jnp.zeros_like(left_t)) for q in range(QUAD)], axis=0
    )
    both = jnp.concatenate([right, turned], axis=1)
    product = jnp.dot(stacked, both, preferred_element_type=jnp.float32)
    for q in range(QUAD):
        for r in range(2):
            planes_ref[pl.ds((first + q * 2 + r) * PAD, BLK), :] = (
                product[q * BLK : (q + 1) * BLK, r * BLK : (r + 1) * BLK] * factors[q]
            )


def bin_factors(pair_ref, count_ref, band, slot, first_bin, segments):
    lo, hi, live = pair_ref[slot, 2, band], pair_ref[slot, 3, band], slot < count_ref[band]
    return [
        jnp.where(
            (lo <= first_bin + q) & (first_bin + q < hi) & live, 1.0 / segments, 0.0
        ).astype(jnp.float32)
        for q in range(QUAD)
    ]


def move_kernel(
    pair_ref, count_ref, strain_ref, table_ref, out_ref, strain, table, rows_ref, own, own_late, gat, late, pick,
    stage, stage_late, got, got_late, planes, tiles, send, recv, send_late, recv_late, load_sem, out_sem,
):
    chunks = own.shape[0]
    tm, band = lax.axis_index("tm"), lax.axis_index("band")
    y, core, x, z = tm // 2, tm % 2, band // SIDE, band % SIDE
    steps = (1, 3, 2)
    moves = [(dv, dy, dc) for dc in (0, 1) for dv in range(SIDE) for dy in range(SIDE)]
    moves = [moves[(11 * k) % len(moves)] for k in range(len(moves))]
    moves = [m for m in moves if m != (0, 0, 0)]

    def around(at, step):
        return lax.rem(at + step, SIDE)

    def on_line(h, place):
        return x * SIDE + place if h == 0 else place * SIDE + z

    def on_cross(h, place):
        return place * SIDE + z if h == 0 else x * SIDE + place

    def mine(h):
        return (z, x) if h == 0 else (x, z)

    def copy(src, dst, c, slot, device):
        return pltpu.make_async_remote_copy(
            src_ref=src,
            dst_ref=dst,
            send_sem=send_late.at[slot] if c is None else send.at[c, slot],
            recv_sem=recv_late.at[slot] if c is None else recv.at[c, slot],
            device_id=device,
            device_id_type=MESH,
        )

    def scatter(c, h):
        out, into = [], []
        v = mine(h)[0]
        for k, d in enumerate(steps):
            to, source = around(v, d), around(v, SIDE - d)
            there = gat.at[c, x, source] if h == 0 else gat.at[c, source, z]
            device = (tm, on_line(h, to))
            out.append((own.at[c, to], gat.at[c, x, z], c, k, device))
            into.append((own.at[c, to], there, c, k, device))
        return out, into

    def gather(c, h):
        out, into = [], []
        w = mine(h)[1]
        for k, d in enumerate(steps):
            here = gat.at[c, x] if h == 0 else gat.at[c, :, z]
            source = around(w, SIDE - d)
            there = gat.at[c, source] if h == 0 else gat.at[c, :, source]
            device = (tm, on_cross(h, around(w, d)))
            out.append((here, here, c, 3 + k, device))
            into.append((there, there, c, 3 + k, device))
        return out, into

    def deal(c, h):
        out, into = [], []
        v = mine(h)[0]
        for k, (dv, dy, dc) in enumerate(moves):
            to_v, to_t = around(v, dv), around(y, dy) * 2 + lax.rem(core + dc, 2)
            from_v = around(v, SIDE - dv)
            from_t = around(y, SIDE - dy) * 2 + lax.rem(core + dc, 2)
            src, device = stage.at[c, to_v, to_t], (to_t, on_line(h, to_v))
            out.append((src, got.at[c, v, tm], c, 6 + k, device))
            into.append((src, got.at[c, from_v, from_t], c, 6 + k, device))
        return out, into

    plane = [(dx, dz) for dz in range(SIDE) for dx in range(SIDE)]
    plane = [plane[(7 * k) % len(plane)] for k in range(len(plane))][1:]

    def scatter_late():
        out, into = [], []
        for k, (dx, dz) in enumerate(plane):
            to = around(x, dx) * SIDE + around(z, dz)
            source = around(x, SIDE - dx) * SIDE + around(z, SIDE - dz)
            here, there = late.at[core, y, pl.ds(band * 2, 2)], late.at[core, y, pl.ds(source * 2, 2)]
            out.append((own_late.at[to], here, None, k, (tm, to)))
            into.append((own_late.at[to], there, None, k, (tm, to)))
        return out, into

    def gather_late():
        out, into = [], []
        for k, d in enumerate(steps):
            here, there = late.at[core, y], late.at[core, around(y, SIDE - d)]
            device = (around(y, d) * 2 + core, band)
            out.append((here, here, None, 15 + k, device))
            into.append((there, there, None, 15 + k, device))
        return out, into

    def swap_late():
        device = (y * 2 + 1 - core, band)
        here, there = late.at[core], late.at[1 - core]
        return [(here, here, None, 18, device)], [(there, there, None, 18, device)]

    def deal_late():
        out, into = [], []
        for k, (dx, dz) in enumerate(plane):
            to = around(x, dx) * SIDE + around(z, dz)
            source = around(x, SIDE - dx) * SIDE + around(z, SIDE - dz)
            out.append((stage_late.at[to], got_late.at[band], None, 19 + k, (tm, to)))
            into.append((stage_late.at[to], got_late.at[source], None, 19 + k, (tm, to)))
        return out, into

    def starts(copies):
        for one in copies:
            copy(*one).start()

    def arrivals(copies):
        for one in copies:
            copy(*one).wait_recv()

    def departures(copies):
        for one in copies:
            copy(*one).wait_send()

    def select(c, h):
        pick[...] = gat[c].reshape(pick.shape)
        for v in range(SIDE):
            owner = on_line(h, v)
            for p in range(stage.shape[2]):
                for w in range(2):
                    stage[c, v, p, w] = pick[pair_ref[p, w, owner]]
        for w in range(2):
            got[c, mine(h)[0], tm, w] = pick[pair_ref[tm, w, band]]

    def select_late():
        for owner in range(SIDE * SIDE):
            for w in range(2):
                stage_late[owner, w] = late[:, :, pair_ref[tm, w, owner]]
        got_late[band] = stage_late[band]

    def write(c, slot):
        rows = tiles.shape[2]
        return pltpu.make_async_copy(
            tiles.at[slot], out_ref.at[:, pl.ds(c * rows, rows), :], out_sem.at[slot]
        )

    def compute(c, after, blocks_of):
        slot = lax.rem(c, 2)
        segments = got.shape[2] * got.shape[5] // QUAD
        for g in range(SIDE):
            factors = bin_factors(pair_ref, count_ref, band, tm, (c * SIDE + g) * QUAD, segments)
            cross_quad(*blocks_of(g), factors, planes, g * QUAD * 2)

        if after is not None:
            write(after, slot).wait()
        rows = tiles.shape[2]
        for a in range(BLK):
            tiles[slot, a] = planes[pl.ds(a, rows, stride=PAD), :].astype(BF)
        write(c, slot).start()

    def chunk_blocks(c):
        def blocks_of(g):
            left, right = got[c, g, :, 0], got[c, g, :, 1]
            turned = jnp.stack([-right[:, 1], right[:, 0]], axis=1)
            return [b.reshape(-1, BLK) for b in (left, right, turned)]

        return blocks_of

    def late_blocks(first):
        def blocks_of(g):
            piece = (first + g) * 2
            left = jnp.stack([got_late[piece, 0], got_late[piece + 1, 0]])
            right = jnp.stack([got_late[piece, 1], got_late[piece + 1, 1]])
            turned = jnp.stack([-right[1], right[0]])
            return [b.reshape(-1, BLK) for b in (left, right, turned)]

        return blocks_of

    loads = [
        pltpu.make_async_copy(strain_ref, strain, load_sem.at[0]),
        pltpu.make_async_copy(table_ref, table, load_sem.at[1]),
    ]
    for load in loads:
        load.start()
    barrier = pltpu.get_barrier_semaphore()
    partners = [(tm, around(x, dx) * SIDE + around(z, dz)) for dx, dz in plane]
    for h in range(2):
        for dv, dy, dc in moves:
            if (dv or h == 0) and (dy or dc):
                to_t = around(y, dy) * 2 + lax.rem(core + dc, 2)
                partners.append((to_t, on_line(h, around(mine(h)[0], dv))))
    for partner in partners:
        pl.semaphore_signal(barrier, inc=1, device_id=partner, device_id_type=MESH)
    for load in loads:
        load.wait()
    whiten(strain, table, own, own_late, rows_ref)
    pl.semaphore_wait(barrier, len(partners))

    def begin(u):
        for h in range(2):
            c = 2 * u + h
            gat[c, x, z] = own[c, mine(h)[0]]
            starts(scatter(c, h)[0])

    def spread(u):
        for h in range(2):
            c = 2 * u + h
            arrivals(scatter(c, h)[1])
            starts(gather(c, h)[0])

    def send_out(u, extra):
        for h in range(2):
            c = 2 * u + h
            arrivals(gather(c, h)[1])
            select(c, h)
            copies = deal(c, h)[0]
            mixed = []
            for k, one in enumerate(copies):
                mixed.append(one)
                mixed += extra[h][k * len(extra[h]) // len(copies) : (k + 1) * len(extra[h]) // len(copies)]
            starts(mixed)

    def finish(u):
        for h in range(2):
            c = 2 * u + h
            arrivals(deal(c, h)[1])
            compute(c, c - 2 if u else None, chunk_blocks(c))

    def settle(u):
        for h in range(2):
            c = 2 * u + h
            departures(scatter(c, h)[0])
            departures(gather(c, h)[0])
            departures(deal(c, h)[0])

    begin(0)
    late[core, y, pl.ds(band * 2, 2)] = own_late[band]
    starts(scatter_late()[0])
    begin(1)
    begin(2)
    spread(0)
    arrivals(scatter_late()[1])
    starts(gather_late()[0])
    send_out(0, ([], []))
    spread(1)
    arrivals(gather_late()[1])
    starts(swap_late()[0])
    spread(2)
    arrivals(swap_late()[1])
    select_late()
    rest = deal_late()[0]
    send_out(1, (rest[0:4], rest[4:8]))
    finish(0)
    send_out(2, (rest[8:11], rest[11:15]))
    settle(0)
    departures(scatter_late()[0])
    departures(gather_late()[0])
    departures(swap_late()[0])
    finish(1)
    settle(1)
    arrivals(deal_late()[1])
    for k in range(2):
        compute(chunks + k, chunks - 4 + k, late_blocks(SIDE * k))
    departures(deal_late()[0])
    for h in range(2):
        c = chunks - 2 + h
        arrivals(deal(c, h)[1])
        compute(c, chunks + h, chunk_blocks(c))
    settle(2)
    for h in range(2):
        write(chunks - 2 + h, h).wait()


def move(pairs, counts, strain_rate):
    segments, channels, samples = strain_rate.shape
    bins, blocks, slots, bands = samples // 2, channels // BLK, 2 * SIDE, SIDE * SIDE
    rows, parts, planes = QUAD * segments, 2, SIDE * QUAD * 2
    pieces = bands
    chunks = (bins // QUAD - pieces // parts) // SIDE
    tile = (rows, BLK)
    return pl.pallas_call(
        move_kernel,
        out_shape=jax.ShapeDtypeStruct((BLK, bins * parts, BLK), BF),
        in_specs=[pl.BlockSpec(memory_space=pltpu.SMEM)] * 2
        + [pl.BlockSpec(memory_space=pl.ANY)] * 2,
        out_specs=pl.BlockSpec(memory_space=pl.ANY),
        scratch_shapes=[
            pltpu.VMEM(strain_rate.shape, BF),
            pltpu.VMEM((samples, samples), BF),
            pltpu.VMEM((parts, bins * segments, BLK), jnp.float32),
            pltpu.VMEM((chunks, SIDE, blocks, parts) + tile, BF),
            pltpu.VMEM((pieces, blocks) + tile, BF),
            pltpu.VMEM((chunks, SIDE, SIDE, blocks, parts) + tile, BF),
            pltpu.VMEM((2, SIDE, bands * blocks) + tile, BF),
            pltpu.VMEM((bands * blocks, parts) + tile, BF),
            pltpu.VMEM((chunks, SIDE, slots, 2, parts) + tile, BF),
            pltpu.VMEM((bands, 2, 2, SIDE) + tile, BF),
            pltpu.VMEM((chunks, SIDE, slots, 2, parts) + tile, BF),
            pltpu.VMEM((pieces, 2, 2, SIDE) + tile, BF),
            pltpu.VMEM((planes * PAD, BLK), jnp.float32),
            pltpu.VMEM((2, BLK, planes, BLK), BF),
            pltpu.SemaphoreType.DMA((chunks, 37)),
            pltpu.SemaphoreType.DMA((chunks, 37)),
            pltpu.SemaphoreType.DMA((34,)),
            pltpu.SemaphoreType.DMA((34,)),
            pltpu.SemaphoreType.DMA((2,)),
            pltpu.SemaphoreType.DMA((2,)),
        ],
        compiler_params=pltpu.CompilerParams(
            collective_id=0, has_side_effects=True, vmem_limit_bytes=24 << 20
        ),
    )(pairs, counts, strain_rate, forward_table(samples))


def lag_kernel(table_ref, cross_ref, out_ref, rows_ref):
    lags, depth = table_ref.shape
    width = cross_ref.shape[0]
    wide = rows_ref.shape[0] // lags
    for a in range(0, width, 2):
        both = jnp.concatenate([cross_ref[a], cross_ref[a + 1]], axis=1)
        lagged = jnp.dot(table_ref[...], both, preferred_element_type=jnp.float32)
        for d in range(2):
            rows_ref[pl.ds(a + d, lags, stride=wide), :] = lagged[:, d * BLK : (d + 1) * BLK]
    out_ref[...] = rows_ref[...].reshape(lags, wide, BLK)[:, :width].astype(BF)


def lag(cross_spec):
    channels, depth, _ = cross_spec.shape
    lags, width = depth, 16
    return pl.pallas_call(
        lag_kernel,
        grid=(channels // width,),
        out_shape=jax.ShapeDtypeStruct((lags, channels, BLK), BF),
        in_specs=[
            pl.BlockSpec((lags, depth), lambda a: (0, 0)),
            pl.BlockSpec((width, depth, BLK), lambda a: (a, 0, 0)),
        ],
        out_specs=pl.BlockSpec((lags, width, BLK), lambda a: (0, a, 0)),
        scratch_shapes=[pltpu.VMEM((lags * (width + 8), BLK), jnp.float32)],
        compiler_params=pltpu.CompilerParams(vmem_limit_bytes=24 << 20),
    )(inverse_table(lags), cross_spec)


def body(strain_rate, pair_table, pair_count):
    pairs = jnp.transpose(pair_table, (1, 2, 0))
    return lag(move(pairs, pair_count, strain_rate))[None, None]


def solution(mesh):
    return jax.shard_map(
        body,
        mesh=mesh,
        in_specs=(P("tm", "band", None), P(), P()),
        out_specs=P("band", "tm", None, None, None),
        check_vma=False,
    )
```

```python
import math

import jax
import jax.numpy as jnp
import numpy as np
from jax import lax
from jax.experimental import pallas as pl
from jax.experimental.pallas import tpu as pltpu
from jax.sharding import PartitionSpec as P

BLK = 128
SUB = 64
EPSILON = 1e-06
MESH = pl.DeviceIdType.MESH
SIDE = 4
QUAD = 4
PAD = 136
BF = jnp.bfloat16


def forward_table(samples):
    n = np.arange(samples)[None, :]
    k = np.arange(samples // 2)[:, None]
    angles = (n * k % samples) * (2.0 * math.pi / samples)
    factor = 1.0 / math.sqrt(samples)
    table = np.concatenate([np.cos(angles) * factor, -np.sin(angles) * factor], axis=0)
    return jnp.asarray(table.astype(np.float32), dtype=BF)


def inverse_table(samples):
    k = np.arange(samples // 2)[None, :]
    t = np.arange(samples)[:, None]
    angles = (t * k % samples) * (2.0 * math.pi / samples)
    factor = 2.0 / math.sqrt(samples // 2)
    table = np.stack([np.cos(angles) * factor, -np.sin(angles) * factor], axis=2)
    return jnp.asarray(table.reshape(samples, samples).astype(np.float32), dtype=BF)


def whiten(strain_ref, table_ref, own, own_late, rows_ref):
    segments, channels, samples = strain_ref.shape
    bins = samples // 2
    chunks, groups = own.shape[:2]
    early = chunks * groups
    for g in range(channels // BLK):
        for s in range(segments):
            x = strain_ref[s, g * BLK : (g + 1) * BLK, :]
            spec = lax.dot_general(
                table_ref[...], x, (((1,), (1,)), ((), ())), preferred_element_type=jnp.float32
            )
            re, im = spec[:bins], spec[bins:]
            power = re * re + im * im
            for m in range(bins // SUB):
                cut = slice(m * SUB, (m + 1) * SUB)
                level = jnp.mean(power[cut], axis=0, keepdims=True)
                scale = 1.0 / jnp.sqrt(level + EPSILON)
                for r, part in enumerate((re, im)):
                    rows_ref[r, pl.ds(m * SUB * segments + s, SUB, stride=segments), :] = (
                        part[cut] * scale
                    )
        for r in range(2):
            tiles = rows_ref[r].reshape(bins // QUAD, QUAD * segments, BLK).astype(BF)
            own[:, :, g, r] = tiles[:early].reshape(chunks, groups, QUAD * segments, BLK)
            for k in range(early, bins // QUAD):
                own_late[(k - early) * 2 + r, g] = tiles[k]


def cross_quad(left, right, turned, factors, planes_ref, first):
    left_t = left.T
    bin_of = lax.broadcasted_iota(jnp.int32, left_t.shape, 1) % 16 // 4
    stacked = jnp.concatenate(
        [jnp.where(bin_of == q, left_t, jnp.zeros_like(left_t)) for q in range(QUAD)], axis=0
    )
    both = jnp.concatenate([right, turned], axis=1)
    product = jnp.dot(stacked, both, preferred_element_type=jnp.float32)
    for q in range(QUAD):
        for r in range(2):
            planes_ref[pl.ds((first + q * 2 + r) * PAD, BLK), :] = (
                product[q * BLK : (q + 1) * BLK, r * BLK : (r + 1) * BLK] * factors[q]
            )


def bin_factors(pair_ref, count_ref, band, slot, first_bin, segments):
    lo, hi, live = pair_ref[slot, 2, band], pair_ref[slot, 3, band], slot < count_ref[band]
    return [
        jnp.where(
            (lo <= first_bin + q) & (first_bin + q < hi) & live, 1.0 / segments, 0.0
        ).astype(jnp.float32)
        for q in range(QUAD)
    ]


def move_kernel(
    pair_ref, count_ref, strain_ref, table_ref, out_ref, strain, table, rows_ref, own, own_late, gat, late, pick,
    stage, stage_late, got, got_late, planes, tiles, send, recv, send_late, recv_late, load_sem, out_sem,
):
    chunks = own.shape[0]
    tm, band = lax.axis_index("tm"), lax.axis_index("band")
    y, core, x, z = tm // 2, tm % 2, band // SIDE, band % SIDE
    steps = (1, 3, 2)
    moves = [(dv, dy, dc) for dc in (0, 1) for dv in range(SIDE) for dy in range(SIDE)]
    moves = [moves[(11 * k) % len(moves)] for k in range(len(moves))]
    moves = [m for m in moves if m != (0, 0, 0)]

    def around(at, step):
        return lax.rem(at + step, SIDE)

    def on_line(h, place):
        return x * SIDE + place if h == 0 else place * SIDE + z

    def on_cross(h, place):
        return place * SIDE + z if h == 0 else x * SIDE + place

    def mine(h):
        return (z, x) if h == 0 else (x, z)

    def copy(src, dst, c, slot, device):
        return pltpu.make_async_remote_copy(
            src_ref=src,
            dst_ref=dst,
            send_sem=send_late.at[slot] if c is None else send.at[c, slot],
            recv_sem=recv_late.at[slot] if c is None else recv.at[c, slot],
            device_id=device,
            device_id_type=MESH,
        )

    def scatter(c, h):
        out, into = [], []
        v = mine(h)[0]
        for k, d in enumerate(steps):
            to, source = around(v, d), around(v, SIDE - d)
            there = gat.at[c, x, source] if h == 0 else gat.at[c, source, z]
            device = (tm, on_line(h, to))
            out.append((own.at[c, to], gat.at[c, x, z], c, k, device))
            into.append((own.at[c, to], there, c, k, device))
        return out, into

    def gather(c, h):
        out, into = [], []
        w = mine(h)[1]
        for k, d in enumerate(steps):
            here = gat.at[c, x] if h == 0 else gat.at[c, :, z]
            source = around(w, SIDE - d)
            there = gat.at[c, source] if h == 0 else gat.at[c, :, source]
            device = (tm, on_cross(h, around(w, d)))
            out.append((here, here, c, 3 + k, device))
            into.append((there, there, c, 3 + k, device))
        return out, into

    def deal(c, h):
        out, into = [], []
        v = mine(h)[0]
        for k, (dv, dy, dc) in enumerate(moves):
            to_v, to_t = around(v, dv), around(y, dy) * 2 + lax.rem(core + dc, 2)
            from_v = around(v, SIDE - dv)
            from_t = around(y, SIDE - dy) * 2 + lax.rem(core + dc, 2)
            src, device = stage.at[c, to_v, to_t], (to_t, on_line(h, to_v))
            out.append((src, got.at[c, v, tm], c, 6 + k, device))
            into.append((src, got.at[c, from_v, from_t], c, 6 + k, device))
        return out, into

    plane = [(dx, dz) for dz in range(SIDE) for dx in range(SIDE)]
    plane = [plane[(7 * k) % len(plane)] for k in range(len(plane))][1:]

    def scatter_late():
        out, into = [], []
        for k, (dx, dz) in enumerate(plane):
            to = around(x, dx) * SIDE + around(z, dz)
            source = around(x, SIDE - dx) * SIDE + around(z, SIDE - dz)
            here, there = late.at[core, y, pl.ds(band * 2, 2)], late.at[core, y, pl.ds(source * 2, 2)]
            out.append((own_late.at[to], here, None, k, (tm, to)))
            into.append((own_late.at[to], there, None, k, (tm, to)))
        return out, into

    def gather_late():
        out, into = [], []
        for k, d in enumerate(steps):
            here, there = late.at[core, y], late.at[core, around(y, SIDE - d)]
            device = (around(y, d) * 2 + core, band)
            out.append((here, here, None, 15 + k, device))
            into.append((there, there, None, 15 + k, device))
        return out, into

    def swap_late():
        device = (y * 2 + 1 - core, band)
        here, there = late.at[core], late.at[1 - core]
        return [(here, here, None, 18, device)], [(there, there, None, 18, device)]

    def deal_late():
        out, into = [], []
        for k, (dx, dz) in enumerate(plane):
            to = around(x, dx) * SIDE + around(z, dz)
            source = around(x, SIDE - dx) * SIDE + around(z, SIDE - dz)
            out.append((stage_late.at[to], got_late.at[band], None, 19 + k, (tm, to)))
            into.append((stage_late.at[to], got_late.at[source], None, 19 + k, (tm, to)))
        return out, into

    def starts(copies):
        for one in copies:
            copy(*one).start()

    def arrivals(copies):
        for one in copies:
            copy(*one).wait_recv()

    def departures(copies):
        for one in copies:
            copy(*one).wait_send()

    def select(c, h):
        pick[...] = gat[c].reshape(pick.shape)
        for v in range(SIDE):
            owner = on_line(h, v)
            for p in range(stage.shape[2]):
                for w in range(2):
                    stage[c, v, p, w] = pick[pair_ref[p, w, owner]]
        for w in range(2):
            got[c, mine(h)[0], tm, w] = pick[pair_ref[tm, w, band]]

    def select_late():
        for owner in range(SIDE * SIDE):
            for w in range(2):
                stage_late[owner, w] = late[:, :, pair_ref[tm, w, owner]]
        got_late[band] = stage_late[band]

    def write(c, slot):
        rows = tiles.shape[2]
        return pltpu.make_async_copy(
            tiles.at[slot], out_ref.at[:, pl.ds(c * rows, rows), :], out_sem.at[slot]
        )

    def compute(c, after, blocks_of):
        slot = lax.rem(c, 2)
        segments = got.shape[2] * got.shape[5] // QUAD
        for g in range(SIDE):
            factors = bin_factors(pair_ref, count_ref, band, tm, (c * SIDE + g) * QUAD, segments)
            cross_quad(*blocks_of(g), factors, planes, g * QUAD * 2)

        if after is not None:
            write(after, slot).wait()
        rows = tiles.shape[2]
        for a in range(BLK):
            tiles[slot, a] = planes[pl.ds(a, rows, stride=PAD), :].astype(BF)
        write(c, slot).start()

    def chunk_blocks(c):
        def blocks_of(g):
            left, right = got[c, g, :, 0], got[c, g, :, 1]
            turned = jnp.stack([-right[:, 1], right[:, 0]], axis=1)
            return [b.reshape(-1, BLK) for b in (left, right, turned)]

        return blocks_of

    def late_blocks(first):
        def blocks_of(g):
            piece = (first + g) * 2
            left = jnp.stack([got_late[piece, 0], got_late[piece + 1, 0]])
            right = jnp.stack([got_late[piece, 1], got_late[piece + 1, 1]])
            turned = jnp.stack([-right[1], right[0]])
            return [b.reshape(-1, BLK) for b in (left, right, turned)]

        return blocks_of

    loads = [
        pltpu.make_async_copy(strain_ref, strain, load_sem.at[0]),
        pltpu.make_async_copy(table_ref, table, load_sem.at[1]),
    ]
    for load in loads:
        load.start()
    barrier = pltpu.get_barrier_semaphore()
    partners = [(tm, around(x, dx) * SIDE + around(z, dz)) for dx, dz in plane]
    for h in range(2):
        for dv, dy, dc in moves:
            if (dv or h == 0) and (dy or dc):
                to_t = around(y, dy) * 2 + lax.rem(core + dc, 2)
                partners.append((to_t, on_line(h, around(mine(h)[0], dv))))
    for partner in partners:
        pl.semaphore_signal(barrier, inc=1, device_id=partner, device_id_type=MESH)
    for load in loads:
        load.wait()
    whiten(strain, table, own, own_late, rows_ref)
    pl.semaphore_wait(barrier, len(partners))

    def begin(u):
        for h in range(2):
            c = 2 * u + h
            gat[c, x, z] = own[c, mine(h)[0]]
            starts(scatter(c, h)[0])

    def spread(u):
        for h in range(2):
            c = 2 * u + h
            arrivals(scatter(c, h)[1])
            starts(gather(c, h)[0])

    def send_out(u, extra):
        for h in range(2):
            c = 2 * u + h
            arrivals(gather(c, h)[1])
            select(c, h)
            copies = deal(c, h)[0]
            mixed = []
            for k, one in enumerate(copies):
                mixed.append(one)
                mixed += extra[h][k * len(extra[h]) // len(copies) : (k + 1) * len(extra[h]) // len(copies)]
            starts(mixed)

    def finish(u):
        for h in range(2):
            c = 2 * u + h
            arrivals(deal(c, h)[1])
            compute(c, c - 2 if u else None, chunk_blocks(c))

    def settle(u):
        for h in range(2):
            c = 2 * u + h
            departures(scatter(c, h)[0])
            departures(gather(c, h)[0])
            departures(deal(c, h)[0])

    late[core, y, pl.ds(band * 2, 2)] = own_late[band]
    starts(scatter_late()[0])
    begin(0)
    arrivals(scatter_late()[1])
    starts(gather_late()[0])
    spread(0)
    begin(1)
    begin(2)
    send_out(0, ([], []))
    spread(1)
    arrivals(gather_late()[1])
    starts(swap_late()[0])
    spread(2)
    arrivals(swap_late()[1])
    select_late()
    rest = deal_late()[0]
    send_out(1, (rest[0:8], rest[8:15]))
    finish(0)
    send_out(2, ([], []))
    settle(0)
    departures(scatter_late()[0])
    departures(gather_late()[0])
    departures(swap_late()[0])
    finish(1)
    settle(1)
    arrivals(deal_late()[1])
    for k in range(2):
        compute(chunks + k, chunks - 4 + k, late_blocks(SIDE * k))
    departures(deal_late()[0])
    for h in range(2):
        c = chunks - 2 + h
        arrivals(deal(c, h)[1])
        compute(c, chunks + h, chunk_blocks(c))
    settle(2)
    for h in range(2):
        write(chunks - 2 + h, h).wait()


def move(pairs, counts, strain_rate):
    segments, channels, samples = strain_rate.shape
    bins, blocks, slots, bands = samples // 2, channels // BLK, 2 * SIDE, SIDE * SIDE
    rows, parts, planes = QUAD * segments, 2, SIDE * QUAD * 2
    pieces = bands
    chunks = (bins // QUAD - pieces // parts) // SIDE
    tile = (rows, BLK)
    return pl.pallas_call(
        move_kernel,
        out_shape=jax.ShapeDtypeStruct((BLK, bins * parts, BLK), BF),
        in_specs=[pl.BlockSpec(memory_space=pltpu.SMEM)] * 2
        + [pl.BlockSpec(memory_space=pl.ANY)] * 2,
        out_specs=pl.BlockSpec(memory_space=pl.ANY),
        scratch_shapes=[
            pltpu.VMEM(strain_rate.shape, BF),
            pltpu.VMEM((samples, samples), BF),
            pltpu.VMEM((parts, bins * segments, BLK), jnp.float32),
            pltpu.VMEM((chunks, SIDE, blocks, parts) + tile, BF),
            pltpu.VMEM((pieces, blocks) + tile, BF),
            pltpu.VMEM((chunks, SIDE, SIDE, blocks, parts) + tile, BF),
            pltpu.VMEM((2, SIDE, bands * blocks) + tile, BF),
            pltpu.VMEM((bands * blocks, parts) + tile, BF),
            pltpu.VMEM((chunks, SIDE, slots, 2, parts) + tile, BF),
            pltpu.VMEM((bands, 2, 2, SIDE) + tile, BF),
            pltpu.VMEM((chunks, SIDE, slots, 2, parts) + tile, BF),
            pltpu.VMEM((pieces, 2, 2, SIDE) + tile, BF),
            pltpu.VMEM((planes * PAD, BLK), jnp.float32),
            pltpu.VMEM((2, BLK, planes, BLK), BF),
            pltpu.SemaphoreType.DMA((chunks, 37)),
            pltpu.SemaphoreType.DMA((chunks, 37)),
            pltpu.SemaphoreType.DMA((34,)),
            pltpu.SemaphoreType.DMA((34,)),
            pltpu.SemaphoreType.DMA((2,)),
            pltpu.SemaphoreType.DMA((2,)),
        ],
        compiler_params=pltpu.CompilerParams(
            collective_id=0, has_side_effects=True, vmem_limit_bytes=24 << 20
        ),
    )(pairs, counts, strain_rate, forward_table(samples))


def lag_kernel(table_ref, cross_ref, out_ref, rows_ref, tiles, out_sem):
    lags = table_ref.shape[0]
    channels, width = cross_ref.shape[0], tiles.shape[2]
    wide = rows_ref.shape[0] // lags
    steps = channels // width

    def write(i, slot):
        return pltpu.make_async_copy(
            tiles.at[slot], out_ref.at[:, pl.ds(i * width, width), :], out_sem.at[slot]
        )

    def step(i, _):
        slot = lax.rem(i, 2)
        for a in range(0, width, 2):
            at = i * width + a
            both = jnp.concatenate([cross_ref[at], cross_ref[at + 1]], axis=1)
            lagged = jnp.dot(table_ref[...], both, preferred_element_type=jnp.float32)
            for d in range(2):
                rows_ref[pl.ds(a + d, lags, stride=wide), :] = lagged[:, d * BLK : (d + 1) * BLK]

        @pl.when(i >= 2)
        def _():
            write(i - 2, slot).wait()

        tiles[slot] = rows_ref[...].reshape(lags, wide, BLK)[:, :width].astype(BF)
        write(i, slot).start()
        return 0

    lax.fori_loop(0, steps, step, 0)
    for i in range(steps - 2, steps):
        write(i, i % 2).wait()


def lag(cross_spec):
    channels, depth, _ = cross_spec.shape
    lags, width = depth, 16
    return pl.pallas_call(
        lag_kernel,
        out_shape=jax.ShapeDtypeStruct((lags, channels, BLK), BF),
        in_specs=[pl.BlockSpec(memory_space=pltpu.VMEM)] * 2,
        out_specs=pl.BlockSpec(memory_space=pl.ANY),
        scratch_shapes=[
            pltpu.VMEM((lags * (width + 8), BLK), jnp.float32),
            pltpu.VMEM((2, lags, width, BLK), BF),
            pltpu.SemaphoreType.DMA((2,)),
        ],
        compiler_params=pltpu.CompilerParams(vmem_limit_bytes=24 << 20),
    )(inverse_table(lags), cross_spec)


def body(strain_rate, pair_table, pair_count):
    pairs = jnp.transpose(pair_table, (1, 2, 0))
    return lag(move(pairs, pair_count, strain_rate))[None, None]


def solution(mesh):
    return jax.shard_map(
        body,
        mesh=mesh,
        in_specs=(P("tm", "band", None), P(), P()),
        out_specs=P("band", "tm", None, None, None),
        check_vma=False,
    )
```

```python
import math

import jax
import jax.numpy as jnp
import numpy as np
from jax import lax
from jax.experimental import pallas as pl
from jax.experimental.pallas import tpu as pltpu
from jax.sharding import PartitionSpec as P

BLK = 128
SUB = 64
EPSILON = 1e-06
MESH = pl.DeviceIdType.MESH
SIDE = 4
QUAD = 4
PAD = 136
BF = jnp.bfloat16


def forward_table(samples):
    n = np.arange(samples)[None, :]
    k = np.arange(samples // 2)[:, None]
    angles = (n * k % samples) * (2.0 * math.pi / samples)
    factor = 1.0 / math.sqrt(samples)
    table = np.concatenate([np.cos(angles) * factor, -np.sin(angles) * factor], axis=0)
    return jnp.asarray(table.astype(np.float32), dtype=BF)


def inverse_table(samples):
    k = np.arange(samples // 2)[None, :]
    t = np.arange(samples)[:, None]
    angles = (t * k % samples) * (2.0 * math.pi / samples)
    factor = 2.0 / math.sqrt(samples // 2)
    table = np.stack([np.cos(angles) * factor, -np.sin(angles) * factor], axis=2)
    return jnp.asarray(table.reshape(samples, samples).astype(np.float32), dtype=BF)


def whiten(strain_ref, table_ref, own, own_late, rows_ref):
    segments, channels, samples = strain_ref.shape
    bins = samples // 2
    chunks, groups = own.shape[:2]
    early = chunks * groups
    for g in range(channels // BLK):
        for s in range(segments):
            x = strain_ref[s, g * BLK : (g + 1) * BLK, :]
            spec = lax.dot_general(
                table_ref[...], x, (((1,), (1,)), ((), ())), preferred_element_type=jnp.float32
            )
            re, im = spec[:bins], spec[bins:]
            power = re * re + im * im
            for m in range(bins // SUB):
                cut = slice(m * SUB, (m + 1) * SUB)
                level = jnp.mean(power[cut], axis=0, keepdims=True)
                scale = 1.0 / jnp.sqrt(level + EPSILON)
                for r, part in enumerate((re, im)):
                    rows_ref[r, pl.ds(m * SUB * segments + s, SUB, stride=segments), :] = (
                        part[cut] * scale
                    )
        for r in range(2):
            tiles = rows_ref[r].reshape(bins // QUAD, QUAD * segments, BLK).astype(BF)
            own[:, :, g, r] = tiles[:early].reshape(chunks, groups, QUAD * segments, BLK)
            for k in range(early, bins // QUAD):
                own_late[(k - early) * 2 + r, g] = tiles[k]


def cross_quad(left, right, turned, factors, planes_ref, first):
    left_t = left.T
    bin_of = lax.broadcasted_iota(jnp.int32, left_t.shape, 1) % 16 // 4
    stacked = jnp.concatenate(
        [jnp.where(bin_of == q, left_t, jnp.zeros_like(left_t)) for q in range(QUAD)], axis=0
    )
    both = jnp.concatenate([right, turned], axis=1)
    product = jnp.dot(stacked, both, preferred_element_type=jnp.float32)
    for q in range(QUAD):
        for r in range(2):
            planes_ref[pl.ds((first + q * 2 + r) * PAD, BLK), :] = (
                product[q * BLK : (q + 1) * BLK, r * BLK : (r + 1) * BLK] * factors[q]
            )


def bin_factors(pair_ref, count_ref, band, slot, first_bin, segments):
    lo, hi, live = pair_ref[slot, 2, band], pair_ref[slot, 3, band], slot < count_ref[band]
    return [
        jnp.where(
            (lo <= first_bin + q) & (first_bin + q < hi) & live, 1.0 / segments, 0.0
        ).astype(jnp.float32)
        for q in range(QUAD)
    ]


def move_kernel(
    pair_ref, count_ref, strain_ref, table_ref, out_ref, strain, table, rows_ref, own, own_late, gat, late, pick,
    stage, stage_late, got, got_late, planes, tiles, send, recv, send_late, recv_late, load_sem, out_sem,
):
    chunks, slots = own.shape[0], pair_ref.shape[0]
    tm, band = lax.axis_index("tm"), lax.axis_index("band")
    y, core, x, z = tm // 2, tm % 2, band // SIDE, band % SIDE
    steps = (1, 3, 2)
    moves = [(dv, dy, dc) for dc in (0, 1) for dv in range(SIDE) for dy in range(SIDE)]
    moves = [moves[(11 * k) % len(moves)] for k in range(len(moves))]
    moves = [m for m in moves if m != (0, 0, 0)]

    def around(at, step):
        return lax.rem(at + step, SIDE)

    def on_line(h, place):
        return x * SIDE + place if h == 0 else place * SIDE + z

    def on_cross(h, place):
        return place * SIDE + z if h == 0 else x * SIDE + place

    def mine(h):
        return (z, x) if h == 0 else (x, z)

    def copy(src, dst, c, slot, device):
        return pltpu.make_async_remote_copy(
            src_ref=src,
            dst_ref=dst,
            send_sem=send_late.at[slot] if c is None else send.at[c, slot],
            recv_sem=recv_late.at[slot] if c is None else recv.at[c, slot],
            device_id=device,
            device_id_type=MESH,
        )

    def scatter(c, h):
        v = mine(h)[0]
        tos = [around(v, d) for d in steps]
        return [(own.at[c, to], gat.at[c, x, z], c, 0, (tm, on_line(h, to))) for to in tos]

    def gather(c, h):
        here = gat.at[c, x] if h == 0 else gat.at[c, :, z]
        return [
            (here, here, c, 1, (tm, on_cross(h, around(mine(h)[1], d)))) for d in steps
        ]

    def deal(c, h):
        out = []
        v = mine(h)[0]
        for dv, dy, dc in moves:
            to_v, to_t = around(v, dv), around(y, dy) * 2 + lax.rem(core + dc, 2)
            src, dst = stage.at[c, to_v * slots + to_t], got.at[c, v * slots + tm]
            out.append((src, dst, c, 2, (to_t, on_line(h, to_v))))
        return out

    plane = [(dx, dz) for dz in range(SIDE) for dx in range(SIDE)]
    plane = [plane[(7 * k) % len(plane)] for k in range(len(plane))][1:]
    over = [around(x, dx) * SIDE + around(z, dz) for dx, dz in plane]

    def scatter_late():
        here = late.at[core, y, pl.ds(band * 2, 2)]
        return [(own_late.at[to], here, None, 0, (tm, to)) for to in over]

    def gather_late():
        here = late.at[core, y]
        return [(here, here, None, 1, (around(y, d) * 2 + core, band)) for d in steps]

    def swap_late():
        here = late.at[core]
        return [(here, here, None, 2, (y * 2 + 1 - core, band))]

    def deal_late():
        return [(stage_late.at[to], got_late.at[band], None, 3, (tm, to)) for to in over]

    def starts(copies):
        for one in copies:
            copy(*one).start()

    def size(c, k):
        if c is None:
            return (
                own_late.at[pl.ds(0, len(over))],
                late.at[0, pl.ds(0, SIDE - 1)],
                late.at[0],
                stage_late.at[pl.ds(0, len(over))],
            )[k]
        return (
            own.at[c, pl.ds(0, SIDE - 1)],
            gat.at[c, pl.ds(0, SIDE - 1)],
            stage.at[c, pl.ds(0, len(moves))],
        )[k]

    def arrivals(c, k):
        sem = recv_late.at[k] if c is None else recv.at[c, k]
        pltpu.make_async_copy(size(c, k), size(c, k), sem).wait()

    def departures(c, k):
        sem = send_late.at[k] if c is None else send.at[c, k]
        pltpu.make_async_copy(size(c, k), size(c, k), sem).wait()

    def select(c, h):
        pick[...] = gat[c].reshape(pick.shape)
        for v in range(SIDE):
            owner = on_line(h, v)
            for p in range(slots):
                for w in range(2):
                    stage[c, v * slots + p, w] = pick[pair_ref[p, w, owner]]
        for w in range(2):
            got[c, mine(h)[0] * slots + tm, w] = pick[pair_ref[tm, w, band]]

    def select_late():
        for owner in range(SIDE * SIDE):
            for w in range(2):
                stage_late[owner, w] = late[:, :, pair_ref[tm, w, owner]]
        got_late[band] = stage_late[band]

    def write(c, slot):
        rows = tiles.shape[2]
        return pltpu.make_async_copy(
            tiles.at[slot], out_ref.at[:, pl.ds(c * rows, rows), :], out_sem.at[slot]
        )

    def compute(c, after, blocks_of):
        slot = lax.rem(c, 2)
        segments = slots * got.shape[4] // QUAD
        for g in range(SIDE):
            factors = bin_factors(pair_ref, count_ref, band, tm, (c * SIDE + g) * QUAD, segments)
            cross_quad(*blocks_of(g), factors, planes, g * QUAD * 2)

        if after is not None:
            write(after, slot).wait()
        rows = tiles.shape[2]
        for a in range(BLK):
            tiles[slot, a] = planes[pl.ds(a, rows, stride=PAD), :].astype(BF)
        write(c, slot).start()

    def chunk_blocks(c):
        def blocks_of(g):
            here = pl.ds(g * slots, slots)
            left, right = got[c, here, 0], got[c, here, 1]
            turned = jnp.stack([-right[:, 1], right[:, 0]], axis=1)
            return [b.reshape(-1, BLK) for b in (left, right, turned)]

        return blocks_of

    def late_blocks(first):
        def blocks_of(g):
            piece = (first + g) * 2
            left = jnp.stack([got_late[piece, 0], got_late[piece + 1, 0]])
            right = jnp.stack([got_late[piece, 1], got_late[piece + 1, 1]])
            turned = jnp.stack([-right[1], right[0]])
            return [b.reshape(-1, BLK) for b in (left, right, turned)]

        return blocks_of

    loads = [
        pltpu.make_async_copy(strain_ref, strain, load_sem.at[0]),
        pltpu.make_async_copy(table_ref, table, load_sem.at[1]),
    ]
    for load in loads:
        load.start()
    barrier = pltpu.get_barrier_semaphore()
    partners = [(tm, to) for to in over]
    for h in range(2):
        for dv, dy, dc in moves:
            if (dv or h == 0) and (dy or dc):
                to_t = around(y, dy) * 2 + lax.rem(core + dc, 2)
                partners.append((to_t, on_line(h, around(mine(h)[0], dv))))
    for partner in partners:
        pl.semaphore_signal(barrier, inc=1, device_id=partner, device_id_type=MESH)
    for load in loads:
        load.wait()
    whiten(strain, table, own, own_late, rows_ref)
    pl.semaphore_wait(barrier, len(partners))

    def begin(u):
        for h in range(2):
            c = 2 * u + h
            gat[c, x, z] = own[c, mine(h)[0]]
            starts(scatter(c, h))

    def spread(u):
        for h in range(2):
            c = 2 * u + h
            arrivals(c, 0)
            starts(gather(c, h))

    def send_out(u, extra):
        for h in range(2):
            c = 2 * u + h
            arrivals(c, 1)
            select(c, h)
            copies = deal(c, h)
            mixed = []
            for k, one in enumerate(copies):
                mixed.append(one)
                mixed += extra[h][k * len(extra[h]) // len(copies) : (k + 1) * len(extra[h]) // len(copies)]
            starts(mixed)

    def finish(u):
        for h in range(2):
            c = 2 * u + h
            arrivals(c, 2)
            compute(c, c - 2 if u else None, chunk_blocks(c))

    def settle(u):
        for h in range(2):
            c = 2 * u + h
            for k in range(3):
                departures(c, k)

    late[core, y, pl.ds(band * 2, 2)] = own_late[band]
    starts(scatter_late())
    begin(0)
    arrivals(None, 0)
    starts(gather_late())
    spread(0)
    begin(1)
    begin(2)
    send_out(0, ([], []))
    spread(1)
    arrivals(None, 1)
    starts(swap_late())
    spread(2)
    arrivals(None, 2)
    select_late()
    rest = deal_late()
    send_out(1, (rest[0:8], rest[8:15]))
    finish(0)
    send_out(2, ([], []))
    settle(0)
    departures(None, 0)
    departures(None, 1)
    departures(None, 2)
    finish(1)
    settle(1)
    arrivals(None, 3)
    for k in range(2):
        compute(chunks + k, chunks - 4 + k, late_blocks(SIDE * k))
    departures(None, 3)
    for h in range(2):
        c = chunks - 2 + h
        arrivals(c, 2)
        compute(c, chunks + h, chunk_blocks(c))
    settle(2)
    for h in range(2):
        write(chunks - 2 + h, h).wait()


def move(pairs, counts, strain_rate):
    segments, channels, samples = strain_rate.shape
    bins, blocks, slots, bands = samples // 2, channels // BLK, 2 * SIDE, SIDE * SIDE
    rows, parts, planes = QUAD * segments, 2, SIDE * QUAD * 2
    pieces = bands
    chunks = (bins // QUAD - pieces // parts) // SIDE
    tile = (rows, BLK)
    return pl.pallas_call(
        move_kernel,
        out_shape=jax.ShapeDtypeStruct((BLK, bins * parts, BLK), BF),
        in_specs=[pl.BlockSpec(memory_space=pltpu.SMEM)] * 2
        + [pl.BlockSpec(memory_space=pl.ANY)] * 2,
        out_specs=pl.BlockSpec(memory_space=pl.ANY),
        scratch_shapes=[
            pltpu.VMEM(strain_rate.shape, BF),
            pltpu.VMEM((samples, samples), BF),
            pltpu.VMEM((parts, bins * segments, BLK), jnp.float32),
            pltpu.VMEM((chunks, SIDE, blocks, parts) + tile, BF),
            pltpu.VMEM((pieces, blocks) + tile, BF),
            pltpu.VMEM((chunks, SIDE, SIDE, blocks, parts) + tile, BF),
            pltpu.VMEM((2, SIDE, bands * blocks) + tile, BF),
            pltpu.VMEM((bands * blocks, parts) + tile, BF),
            pltpu.VMEM((chunks, SIDE * slots, 2, parts) + tile, BF),
            pltpu.VMEM((bands, 2, 2, SIDE) + tile, BF),
            pltpu.VMEM((chunks, SIDE * slots, 2, parts) + tile, BF),
            pltpu.VMEM((pieces, 2, 2, SIDE) + tile, BF),
            pltpu.VMEM((planes * PAD, BLK), jnp.float32),
            pltpu.VMEM((2, BLK, planes, BLK), BF),
            pltpu.SemaphoreType.DMA((chunks, 3)),
            pltpu.SemaphoreType.DMA((chunks, 3)),
            pltpu.SemaphoreType.DMA((4,)),
            pltpu.SemaphoreType.DMA((4,)),
            pltpu.SemaphoreType.DMA((2,)),
            pltpu.SemaphoreType.DMA((2,)),
        ],
        compiler_params=pltpu.CompilerParams(
            collective_id=0, has_side_effects=True, vmem_limit_bytes=24 << 20
        ),
    )(pairs, counts, strain_rate, forward_table(samples))


def lag_kernel(table_ref, cross_ref, out_ref, rows_ref, tiles, out_sem):
    lags = table_ref.shape[0]
    channels, width = cross_ref.shape[0], tiles.shape[2]
    wide = rows_ref.shape[0] // lags
    steps = channels // width

    def write(i, slot):
        return pltpu.make_async_copy(
            tiles.at[slot], out_ref.at[:, pl.ds(i * width, width), :], out_sem.at[slot]
        )

    def step(i, _):
        slot = lax.rem(i, 2)
        for a in range(0, width, 2):
            at = i * width + a
            both = jnp.concatenate([cross_ref[at], cross_ref[at + 1]], axis=1)
            lagged = jnp.dot(table_ref[...], both, preferred_element_type=jnp.float32)
            for d in range(2):
                rows_ref[pl.ds(a + d, lags, stride=wide), :] = lagged[:, d * BLK : (d + 1) * BLK]

        @pl.when(i >= 2)
        def _():
            write(i - 2, slot).wait()

        tiles[slot] = rows_ref[...].reshape(lags, wide, BLK)[:, :width].astype(BF)
        write(i, slot).start()
        return 0

    lax.fori_loop(0, steps, step, 0)
    for i in range(steps - 2, steps):
        write(i, i % 2).wait()


def lag(cross_spec):
    channels, depth, _ = cross_spec.shape
    lags, width = depth, 16
    return pl.pallas_call(
        lag_kernel,
        out_shape=jax.ShapeDtypeStruct((lags, channels, BLK), BF),
        in_specs=[pl.BlockSpec(memory_space=pltpu.VMEM)] * 2,
        out_specs=pl.BlockSpec(memory_space=pl.ANY),
        scratch_shapes=[
            pltpu.VMEM((lags * (width + 8), BLK), jnp.float32),
            pltpu.VMEM((2, lags, width, BLK), BF),
            pltpu.SemaphoreType.DMA((2,)),
        ],
        compiler_params=pltpu.CompilerParams(vmem_limit_bytes=24 << 20),
    )(inverse_table(lags), cross_spec)


def body(strain_rate, pair_table, pair_count):
    pairs = jnp.transpose(pair_table, (1, 2, 0))
    return lag(move(pairs, pair_count, strain_rate))[None, None]


def solution(mesh):
    return jax.shard_map(
        body,
        mesh=mesh,
        in_specs=(P("tm", "band", None), P(), P()),
        out_specs=P("band", "tm", None, None, None),
        check_vma=False,
    )
```

```python
import math

import jax
import jax.numpy as jnp
import numpy as np
from jax import lax
from jax.experimental import pallas as pl
from jax.experimental.pallas import tpu as pltpu
from jax.sharding import PartitionSpec as P

BLK = 128
SUB = 64
EPSILON = 1e-06
MESH = pl.DeviceIdType.MESH
SIDE = 4
QUAD = 4
PAD = 136
BF = jnp.bfloat16


def forward_table(samples):
    n = np.arange(samples)[None, :]
    k = np.arange(samples // 2)[:, None]
    angles = (n * k % samples) * (2.0 * math.pi / samples)
    factor = 1.0 / math.sqrt(samples)
    table = np.concatenate([np.cos(angles) * factor, -np.sin(angles) * factor], axis=0)
    return jnp.asarray(table.astype(np.float32), dtype=BF)


def inverse_table(samples):
    k = np.arange(samples // 2)[None, :]
    t = np.arange(samples)[:, None]
    angles = (t * k % samples) * (2.0 * math.pi / samples)
    factor = 2.0 / math.sqrt(samples // 2)
    table = np.stack([np.cos(angles) * factor, -np.sin(angles) * factor], axis=2)
    return jnp.asarray(table.reshape(samples, samples).astype(np.float32), dtype=BF)


def whiten(strain_ref, table_ref, own, own_late, rows_ref):
    segments, channels, samples = strain_ref.shape
    bins = samples // 2
    chunks, groups = own.shape[:2]
    early = chunks * groups
    for g in range(channels // BLK):
        for s in range(segments):
            x = strain_ref[s, g * BLK : (g + 1) * BLK, :]
            spec = lax.dot_general(
                table_ref[...], x, (((1,), (1,)), ((), ())), preferred_element_type=jnp.float32
            )
            re, im = spec[:bins], spec[bins:]
            power = re * re + im * im
            for m in range(bins // SUB):
                cut = slice(m * SUB, (m + 1) * SUB)
                level = jnp.mean(power[cut], axis=0, keepdims=True)
                scale = 1.0 / jnp.sqrt(level + EPSILON)
                for r, part in enumerate((re, im)):
                    rows_ref[r, pl.ds(m * SUB * segments + s, SUB, stride=segments), :] = (
                        part[cut] * scale
                    )
        for r in range(2):
            tiles = rows_ref[r].reshape(bins // QUAD, QUAD * segments, BLK).astype(BF)
            own[:, :, g, r] = tiles[:early].reshape(chunks, groups, QUAD * segments, BLK)
            for k in range(early, bins // QUAD):
                own_late[(k - early) * 2 + r, g] = tiles[k]


def cross_quad(left, right, turned, factors, planes_ref, first):
    left_t = left.T
    bin_of = lax.broadcasted_iota(jnp.int32, left_t.shape, 1) % 16 // 4
    stacked = jnp.concatenate(
        [jnp.where(bin_of == q, left_t, jnp.zeros_like(left_t)) for q in range(QUAD)], axis=0
    )
    both = jnp.concatenate([right, turned], axis=1)
    product = jnp.dot(stacked, both, preferred_element_type=jnp.float32)
    for q in range(QUAD):
        for r in range(2):
            planes_ref[pl.ds((first + q * 2 + r) * PAD, BLK), :] = (
                product[q * BLK : (q + 1) * BLK, r * BLK : (r + 1) * BLK] * factors[q]
            )


def bin_factors(pair_ref, count_ref, band, slot, first_bin, segments):
    lo, hi, live = pair_ref[slot, 2, band], pair_ref[slot, 3, band], slot < count_ref[band]
    return [
        jnp.where(
            (lo <= first_bin + q) & (first_bin + q < hi) & live, 1.0 / segments, 0.0
        ).astype(jnp.float32)
        for q in range(QUAD)
    ]


def move_kernel(
    pair_ref, count_ref, strain_ref, table_ref, out_ref, rows_ref, own, own_late, gat, late, pick,
    stage, stage_late, got, got_late, planes, tiles, send, recv, send_late, recv_late, out_sem,
):
    chunks, slots = own.shape[0], pair_ref.shape[0]
    tm, band = lax.axis_index("tm"), lax.axis_index("band")
    y, core, x, z = tm // 2, tm % 2, band // SIDE, band % SIDE
    steps = (1, 3, 2)
    moves = [(dv, dy, dc) for dc in (0, 1) for dv in range(SIDE) for dy in range(SIDE)]
    moves = [moves[(11 * k) % len(moves)] for k in range(len(moves))]
    moves = [m for m in moves if m != (0, 0, 0)]

    def around(at, step):
        return lax.rem(at + step, SIDE)

    def on_line(h, place):
        return x * SIDE + place if h == 0 else place * SIDE + z

    def on_cross(h, place):
        return place * SIDE + z if h == 0 else x * SIDE + place

    def mine(h):
        return (z, x) if h == 0 else (x, z)

    def copy(src, dst, c, slot, device):
        return pltpu.make_async_remote_copy(
            src_ref=src,
            dst_ref=dst,
            send_sem=send_late.at[slot] if c is None else send.at[c, slot],
            recv_sem=recv_late.at[slot] if c is None else recv.at[c, slot],
            device_id=device,
            device_id_type=MESH,
        )

    def scatter(c, h):
        v = mine(h)[0]
        tos = [around(v, d) for d in steps]
        return [(own.at[c, to], gat.at[c, x, z], c, 0, (tm, on_line(h, to))) for to in tos]

    def gather(c, h):
        here = gat.at[c, x] if h == 0 else gat.at[c, :, z]
        return [
            (here, here, c, 1, (tm, on_cross(h, around(mine(h)[1], d)))) for d in steps
        ]

    def deal(c, h):
        out = []
        v = mine(h)[0]
        for dv, dy, dc in moves:
            to_v, to_t = around(v, dv), around(y, dy) * 2 + lax.rem(core + dc, 2)
            src, dst = stage.at[c, to_v * slots + to_t], got.at[c, v * slots + tm]
            out.append((src, dst, c, 2, (to_t, on_line(h, to_v))))
        return out

    plane = [(dx, dz) for dz in range(SIDE) for dx in range(SIDE)]
    plane = [plane[(7 * k) % len(plane)] for k in range(len(plane))][1:]
    over = [around(x, dx) * SIDE + around(z, dz) for dx, dz in plane]

    def scatter_late():
        here = late.at[core, y, pl.ds(band * 2, 2)]
        return [(own_late.at[to], here, None, 0, (tm, to)) for to in over]

    def gather_late():
        here = late.at[core, y]
        return [(here, here, None, 1, (around(y, d) * 2 + core, band)) for d in steps]

    def swap_late():
        here = late.at[core]
        return [(here, here, None, 2, (y * 2 + 1 - core, band))]

    def deal_late():
        return [(stage_late.at[to], got_late.at[band], None, 3, (tm, to)) for to in over]

    def starts(copies):
        for one in copies:
            copy(*one).start()

    def size(c, k):
        if c is None:
            return (
                own_late.at[pl.ds(0, len(over))],
                late.at[0, pl.ds(0, SIDE - 1)],
                late.at[0],
                stage_late.at[pl.ds(0, len(over))],
            )[k]
        return (
            own.at[c, pl.ds(0, SIDE - 1)],
            gat.at[c, pl.ds(0, SIDE - 1)],
            stage.at[c, pl.ds(0, len(moves))],
        )[k]

    def arrivals(c, k):
        sem = recv_late.at[k] if c is None else recv.at[c, k]
        pltpu.make_async_copy(size(c, k), size(c, k), sem).wait()

    def departures(c, k):
        sem = send_late.at[k] if c is None else send.at[c, k]
        pltpu.make_async_copy(size(c, k), size(c, k), sem).wait()

    def select(c, h):
        pick[...] = gat[c].reshape(pick.shape)
        for v in range(SIDE):
            owner = on_line(h, v)
            for p in range(slots):
                for w in range(2):
                    stage[c, v * slots + p, w] = pick[pair_ref[p, w, owner]]
        for w in range(2):
            got[c, mine(h)[0] * slots + tm, w] = pick[pair_ref[tm, w, band]]

    def select_late():
        for owner in range(SIDE * SIDE):
            for w in range(2):
                stage_late[owner, w] = late[:, :, pair_ref[tm, w, owner]]
        got_late[band] = stage_late[band]

    def write(c, slot):
        rows = tiles.shape[2]
        return pltpu.make_async_copy(
            tiles.at[slot], out_ref.at[:, pl.ds(c * rows, rows), :], out_sem.at[slot]
        )

    def compute(c, after, blocks_of):
        slot = lax.rem(c, 2)
        segments = slots * got.shape[4] // QUAD
        for g in range(SIDE):
            factors = bin_factors(pair_ref, count_ref, band, tm, (c * SIDE + g) * QUAD, segments)
            cross_quad(*blocks_of(g), factors, planes, g * QUAD * 2)

        if after is not None:
            write(after, slot).wait()
        rows = tiles.shape[2]
        for a in range(BLK):
            tiles[slot, a] = planes[pl.ds(a, rows, stride=PAD), :].astype(BF)
        write(c, slot).start()

    def chunk_blocks(c):
        def blocks_of(g):
            here = pl.ds(g * slots, slots)
            left, right = got[c, here, 0], got[c, here, 1]
            turned = jnp.stack([-right[:, 1], right[:, 0]], axis=1)
            return [b.reshape(-1, BLK) for b in (left, right, turned)]

        return blocks_of

    def late_blocks(first):
        def blocks_of(g):
            piece = (first + g) * 2
            left = jnp.stack([got_late[piece, 0], got_late[piece + 1, 0]])
            right = jnp.stack([got_late[piece, 1], got_late[piece + 1, 1]])
            turned = jnp.stack([-right[1], right[0]])
            return [b.reshape(-1, BLK) for b in (left, right, turned)]

        return blocks_of

    barrier = pltpu.get_barrier_semaphore()
    partners = [(tm, to) for to in over]
    for h in range(2):
        for dv, dy, dc in moves:
            if (dv or h == 0) and (dy or dc):
                to_t = around(y, dy) * 2 + lax.rem(core + dc, 2)
                partners.append((to_t, on_line(h, around(mine(h)[0], dv))))
    for partner in partners:
        pl.semaphore_signal(barrier, inc=1, device_id=partner, device_id_type=MESH)
    whiten(strain_ref, table_ref, own, own_late, rows_ref)
    pl.semaphore_wait(barrier, len(partners))

    def begin(u):
        for h in range(2):
            c = 2 * u + h
            gat[c, x, z] = own[c, mine(h)[0]]
            starts(scatter(c, h))

    def spread(u):
        for h in range(2):
            c = 2 * u + h
            arrivals(c, 0)
            starts(gather(c, h))

    def send_out(u, extra):
        for h in range(2):
            c = 2 * u + h
            arrivals(c, 1)
            select(c, h)
            copies = deal(c, h)
            mixed = []
            for k, one in enumerate(copies):
                mixed.append(one)
                mixed += extra[h][k * len(extra[h]) // len(copies) : (k + 1) * len(extra[h]) // len(copies)]
            starts(mixed)

    def finish(u):
        for h in range(2):
            c = 2 * u + h
            arrivals(c, 2)
            compute(c, c - 2 if u else None, chunk_blocks(c))

    def settle(u):
        for h in range(2):
            c = 2 * u + h
            for k in range(3):
                departures(c, k)

    late[core, y, pl.ds(band * 2, 2)] = own_late[band]
    starts(scatter_late())
    begin(0)
    arrivals(None, 0)
    starts(gather_late())
    spread(0)
    begin(1)
    begin(2)
    send_out(0, ([], []))
    spread(1)
    arrivals(None, 1)
    starts(swap_late())
    spread(2)
    arrivals(None, 2)
    select_late()
    rest = deal_late()
    send_out(1, (rest[0:8], rest[8:15]))
    finish(0)
    send_out(2, ([], []))
    settle(0)
    departures(None, 0)
    departures(None, 1)
    departures(None, 2)
    finish(1)
    settle(1)
    arrivals(None, 3)
    for k in range(2):
        compute(chunks + k, chunks - 4 + k, late_blocks(SIDE * k))
    departures(None, 3)
    for h in range(2):
        c = chunks - 2 + h
        arrivals(c, 2)
        compute(c, chunks + h, chunk_blocks(c))
    settle(2)
    for h in range(2):
        write(chunks - 2 + h, h).wait()


def move(pairs, counts, strain_rate):
    segments, channels, samples = strain_rate.shape
    bins, blocks, slots, bands = samples // 2, channels // BLK, 2 * SIDE, SIDE * SIDE
    rows, parts, planes = QUAD * segments, 2, SIDE * QUAD * 2
    pieces = bands
    chunks = (bins // QUAD - pieces // parts) // SIDE
    tile = (rows, BLK)
    return pl.pallas_call(
        move_kernel,
        out_shape=jax.ShapeDtypeStruct((BLK, bins * parts, BLK), BF),
        in_specs=[pl.BlockSpec(memory_space=pltpu.SMEM)] * 2
        + [pl.BlockSpec(memory_space=pltpu.VMEM)] * 2,
        out_specs=pl.BlockSpec(memory_space=pl.ANY),
        scratch_shapes=[
            pltpu.VMEM((parts, bins * segments, BLK), jnp.float32),
            pltpu.VMEM((chunks, SIDE, blocks, parts) + tile, BF),
            pltpu.VMEM((pieces, blocks) + tile, BF),
            pltpu.VMEM((chunks, SIDE, SIDE, blocks, parts) + tile, BF),
            pltpu.VMEM((2, SIDE, bands * blocks) + tile, BF),
            pltpu.VMEM((bands * blocks, parts) + tile, BF),
            pltpu.VMEM((chunks, SIDE * slots, 2, parts) + tile, BF),
            pltpu.VMEM((bands, 2, 2, SIDE) + tile, BF),
            pltpu.VMEM((chunks, SIDE * slots, 2, parts) + tile, BF),
            pltpu.VMEM((pieces, 2, 2, SIDE) + tile, BF),
            pltpu.VMEM((planes * PAD, BLK), jnp.float32),
            pltpu.VMEM((2, BLK, planes, BLK), BF),
            pltpu.SemaphoreType.DMA((chunks, 3)),
            pltpu.SemaphoreType.DMA((chunks, 3)),
            pltpu.SemaphoreType.DMA((4,)),
            pltpu.SemaphoreType.DMA((4,)),
            pltpu.SemaphoreType.DMA((2,)),
        ],
        compiler_params=pltpu.CompilerParams(
            collective_id=0, has_side_effects=True, vmem_limit_bytes=24 << 20
        ),
    )(pairs, counts, strain_rate, forward_table(samples))


def lag_kernel(table_ref, cross_ref, out_ref, rows_ref, tiles, out_sem):
    lags = table_ref.shape[0]
    channels, width = cross_ref.shape[0], tiles.shape[2]
    wide = rows_ref.shape[0] // lags
    steps = channels // width

    def write(i, slot):
        return pltpu.make_async_copy(
            tiles.at[slot], out_ref.at[:, pl.ds(i * width, width), :], out_sem.at[slot]
        )

    def step(i, _):
        slot = lax.rem(i, 2)
        for a in range(0, width, 2):
            at = i * width + a
            both = jnp.concatenate([cross_ref[at], cross_ref[at + 1]], axis=1)
            lagged = jnp.dot(table_ref[...], both, preferred_element_type=jnp.float32)
            for d in range(2):
                rows_ref[pl.ds(a + d, lags, stride=wide), :] = lagged[:, d * BLK : (d + 1) * BLK]

        @pl.when(i >= 2)
        def _():
            write(i - 2, slot).wait()

        tiles[slot] = rows_ref[...].reshape(lags, wide, BLK)[:, :width].astype(BF)
        write(i, slot).start()
        return 0

    lax.fori_loop(0, steps, step, 0)
    for i in range(steps - 2, steps):
        write(i, i % 2).wait()


def lag(cross_spec):
    channels, depth, _ = cross_spec.shape
    lags, width = depth, 16
    return pl.pallas_call(
        lag_kernel,
        out_shape=jax.ShapeDtypeStruct((lags, channels, BLK), BF),
        in_specs=[pl.BlockSpec(memory_space=pltpu.VMEM)] * 2,
        out_specs=pl.BlockSpec(memory_space=pl.ANY),
        scratch_shapes=[
            pltpu.VMEM((lags * (width + 8), BLK), jnp.float32),
            pltpu.VMEM((2, lags, width, BLK), BF),
            pltpu.SemaphoreType.DMA((2,)),
        ],
        compiler_params=pltpu.CompilerParams(vmem_limit_bytes=24 << 20),
    )(inverse_table(lags), cross_spec)


def body(strain_rate, pair_table, pair_count):
    pairs = jnp.transpose(pair_table, (1, 2, 0))
    return lag(move(pairs, pair_count, strain_rate))[None, None]


def solution(mesh):
    return jax.shard_map(
        body,
        mesh=mesh,
        in_specs=(P("tm", "band", None), P(), P()),
        out_specs=P("band", "tm", None, None, None),
        check_vma=False,
    )
```
